256 devices in a mesh: sky: 16 (over x, y), freq: 16 (over z, core).
Axes of the slice: x: 4, y: 4, z: 8, core: 2. Of those that a mesh axis runs over, the one named last changes fastest.
Arguments:
- pieces: bfloat16 [128, 128, 128, 128], P('sky', 'freq'), may hold values from -120 to 120
- beam: bfloat16 [128, 128, 128], P('sky'), may hold values from 0.099609375 to 1
- destination: int32 [128], P('sky'), may hold values from 0 to 63, as said below
- clip_tenths: int32 [3, 4], replicated, may hold values from 30 to 60
Outputs:
- significance: float32 [128, 2048, 512], P('freq', 'sky')
The draws below stay inside these ranges and needn't reach their ends.
Inputs may be any that keep to these rules, and one draw needn't show every extreme that they name: Among the 8 pieces of one index of sky, at most 2 have destinations in one tile, that is with equal destination // 4. In every draw some tile receives exactly 2 pieces from every index of sky.
All inputs are finite; a program needn't handle non-finite values.
Results may differ from the reference program's by a relative error of at most 0.0036.
Values may be sent and summed in bfloat16 or wider, within the bound.
A program may use at most 128 MiB of HBM per device.

```python
import functools
import math
import jax
import jax.numpy as jnp
from jax import lax

BLK = 128
ROWB = 1
COLB = 4
RIM = 8
EDGE = 7
KERNELS = 3
WIDTHS = 4
PC_DEV = 8
CAP = 2
PIECES = 128
CH = 128
NY = 2048
NX = 512
BLOCKS = 64
N_SKY = 16


def routing(key):
    owners = PIECES // PC_DEV
    tile_blocks = ROWB * COLB
    busiest = jax.random.randint(jax.random.fold_in(key, 101), (), 0, owners)

    def source(source_index):
        source_key = jax.random.fold_in(jax.random.fold_in(key, 202), source_index)
        spread = jax.random.permutation(jax.random.fold_in(source_key, 1), (owners - 1) * CAP)[:PC_DEV - CAP] // CAP
        spread = spread.astype(jnp.int32)
        spread = spread + (spread >= busiest).astype(jnp.int32)
        chosen = jnp.concatenate([jnp.full((CAP,), busiest, jnp.int32), spread])
        shuffle = jax.random.permutation(jax.random.fold_in(source_key, 2), PC_DEV)
        chosen = chosen[shuffle]
        within = jax.random.randint(jax.random.fold_in(source_key, 3), (PC_DEV,), 0, tile_blocks)
        return chosen * tile_blocks + within
    return jax.vmap(source)(jnp.arange(owners)).reshape(PIECES).astype(jnp.int32)


def draw_destination(key, part):
    return routing(key)


def spread_groups(grouped):
    return jnp.repeat(grouped, 8, axis=1)[:, :CH]


def draw_pieces(key, part):
    targets = routing(key)
    owners = PIECES // PC_DEV
    owner_tile = (targets // (ROWB * COLB)).astype(jnp.float32)
    position = owner_tile / float(max(owners - 1, 1))
    groups = (CH + 7) // 8
    group_shape = (PIECES, groups, BLK, BLK)
    shape = (PIECES, CH, BLK, BLK)
    shared_key = jax.random.fold_in(key, 404)
    own_key = jax.random.fold_in(key, 405)
    brightness = 1.0 + 2.0 * position
    limit = 4.0
    background = 0.012
    lowest = 1.8
    highest = 3.0
    shared = jnp.clip(jax.random.normal(shared_key, group_shape, jnp.float32), -4.0, 4.0)
    own = jnp.clip(jax.random.normal(own_key, shape, jnp.float32), -4.0, 4.0)
    present = jax.random.bernoulli(jax.random.fold_in(key, 406), 1.0 / 32768.0, group_shape).astype(jnp.float32)
    signs = jnp.where(jax.random.bernoulli(jax.random.fold_in(key, 407), 0.5, group_shape), 1.0, -1.0)
    amplitude = jax.random.uniform(jax.random.fold_in(key, 408), group_shape, jnp.float32, lowest, highest) * signs * present
    cluster = amplitude + 0.6 * jnp.roll(amplitude, 1, axis=3) + 0.4 * jnp.roll(amplitude, 1, axis=2)
    base = spread_groups(cluster) + background * (0.9 * spread_groups(shared) + 0.45 * own)
    base = jnp.clip(base, -limit, limit)
    channel_scale = jnp.exp(jax.random.uniform(jax.random.fold_in(key, 303), (CH,), jnp.float32, 0.0, math.log(10.0)))
    return (base * brightness[:, None, None, None] * channel_scale[None, :, None, None]).astype(jnp.bfloat16)


def place_ends(entries, stream_key, least, top_value):
    longest = entries.shape.index(max(entries.shape))
    spots = []
    for shift in (0, 1):
        where = [jax.random.randint(jax.random.fold_in(stream_key, axis), (), 0, length) for axis, length in enumerate(entries.shape)]
        where[longest] = (where[longest] + shift) % entries.shape[longest]
        spots.append(tuple(where))
    return entries.at[spots[0]].set(least).at[spots[1]].set(top_value)


def levels(stream_key, extent, shards, smallest, high):
    factor_of = 1.0
    for dim, blocks in shards:
        draws = jax.random.uniform(jax.random.fold_in(jax.random.fold_in(stream_key, 6), dim), (blocks,), jnp.float32, smallest / len(shards), high / len(shards))
        factor_of = factor_of * jnp.repeat(jnp.exp(draws), extent[dim] // blocks).reshape((-1,) + (1,) * (len(extent) - 1 - dim))
    return factor_of


def setup_inputs(seed: int = 0) -> dict:
    seeds = jax.random.split(jax.random.key(seed), 5)
    pieces = draw_pieces(jax.random.fold_in(seeds[4], 71), 0)
    beam = jnp.clip(jnp.exp(math.log(1.0) - 2.306499 * jax.random.uniform(seeds[1], (PIECES, BLK, BLK), jnp.float32) ** levels(seeds[1], (PIECES, BLK, BLK), ((0, 16),), -0.2, 0.2)), 0.099609375, 1.0).astype(jnp.bfloat16)
    destination = draw_destination(jax.random.fold_in(seeds[4], 71), 0)
    clip_tenths = place_ends(jax.random.randint(seeds[3], (KERNELS, WIDTHS), 30, 61), jax.random.fold_in(seeds[3], 1), 30, 60).astype(jnp.int32)
    return dict(pieces=pieces, beam=beam, destination=destination, clip_tenths=clip_tenths)


REGULARIZER = 0.05
EPSILON = 1e-06
KERNEL_FWHM = (3.0, 6.0, 9.0)
HALF_WIDTHS = (0, 1, 3, 7)

def kernel_taps(kernel):
    offsets = jnp.arange(-RIM, RIM + 1).astype(jnp.float32)
    sigma = KERNEL_FWHM[kernel] / 2.3548
    values = jnp.exp(-offsets * offsets / (2.0 * sigma * sigma))
    return lax.optimization_barrier(values.astype(jnp.bfloat16)).astype(jnp.float32)

def smooth_plane(weights, channel_plane):
    widened = jnp.pad(channel_plane.astype(jnp.float32), ((0, 0), (RIM, RIM)))
    across = jnp.zeros((NY, NX), jnp.float32)
    for offset in range(2 * RIM + 1):
        across = across + weights[offset] * widened[:, offset:offset + NX]
    across = lax.optimization_barrier(across.astype(jnp.bfloat16)).astype(jnp.float32)
    taller = jnp.pad(across, ((RIM, RIM), (0, 0)))
    result = jnp.zeros((NY, NX), jnp.float32)
    for offset in range(2 * RIM + 1):
        result = result + weights[offset] * taller[offset:offset + NY, :]
    return result.astype(jnp.bfloat16)

def boxcars(layer, channel):
    window = lax.dynamic_slice_in_dim(layer, channel, 2 * EDGE + 1, 0).astype(jnp.float32)
    running = window[EDGE]
    found = [running]
    for step in range(1, EDGE + 1):
        running = running + window[EDGE - step] + window[EDGE + step]
        if step in HALF_WIDTHS:
            found.append(running)
    return found

def reference(pieces, beam, destination, clip_tenths):
    beam_wide = beam.astype(jnp.float32)
    coverage = jax.ops.segment_sum(beam_wide * beam_wide, destination, num_segments=BLOCKS) + REGULARIZER

    def combined_plane(channel_pieces):
        weighted = lax.optimization_barrier((beam_wide * channel_pieces.astype(jnp.float32)).astype(jnp.bfloat16)).astype(jnp.float32)
        numerator = jax.ops.segment_sum(weighted, destination, num_segments=BLOCKS)
        blocks = (numerator / coverage).astype(jnp.bfloat16)
        arranged = blocks.reshape(N_SKY, ROWB, COLB, BLK, BLK).transpose(0, 1, 3, 2, 4)
        return arranged.reshape(NY, NX)
    combined = lax.map(combined_plane, jnp.moveaxis(pieces, 1, 0))
    padded = []
    for kernel in range(KERNELS):
        weights = kernel_taps(kernel)
        smoothed = lax.map(functools.partial(smooth_plane, weights), combined)
        padded.append(jnp.pad(smoothed, ((EDGE, EDGE), (0, 0), (0, 0))))

    def channel_power(channel):
        rows_out = []
        for layer in padded:
            rows_out.append(jnp.stack([jnp.sum(found * found) for found in boxcars(layer, channel)]))
        return jnp.stack(rows_out)
    channels = jnp.arange(CH).astype(jnp.int32)
    powers = lax.map(channel_power, channels)
    noise_level = jnp.sqrt(powers / float(NY * NX) + EPSILON)
    factor = 10.0 / (clip_tenths.astype(jnp.float32)[None] * noise_level)

    def channel_score(inputs):
        channel, scales = inputs
        best = jnp.zeros((NY, NX), jnp.float32)
        for kernel in range(KERNELS):
            for width, running in enumerate(boxcars(padded[kernel], channel)):
                best = jnp.maximum(best, jnp.abs(running) * scales[kernel, width])
        return best
    return lax.map(channel_score, (channels, factor))
```

```python
import functools
import numpy as np
import ml_dtypes
import jax
import jax.numpy as jnp
from jax import lax
from jax.experimental import pallas as pl
from jax.experimental.pallas import tpu as pltpu
from jax.sharding import PartitionSpec as P

ROWB = 1
COLB = 4
BLK = 128
RIM = 8
EDGE = 7
KERNELS = 3
WIDTHS = 4
NEAR = 16
REGULARIZER = 0.05
EPSILON = 1e-06
KERNEL_FWHM = (3.0, 6.0, 9.0)
HALF_WIDTHS = (0, 1, 3, 7)
CELLS = 2048 * 512
MESH = pl.DeviceIdType.MESH
VMEM = pltpu.VMEM
F32 = jnp.float32
BF16 = jnp.bfloat16


def band_constants():
    across, down = [], []
    for fwhm in KERNEL_FWHM:
        offsets = np.arange(-RIM, RIM + 1).astype(np.float32)
        sigma = np.float32(fwhm / 2.3548)
        taps = np.exp(-offsets * offsets / (np.float32(2.0) * sigma * sigma)).astype(ml_dtypes.bfloat16)

        def pick(distance):
            inside = np.abs(distance) <= RIM
            return np.where(inside, taps[np.clip(distance + RIM, 0, 2 * RIM)], taps.dtype.type(0))

        columns = np.arange(COLB * BLK)
        across.append(pick(columns[:, None] - columns[None, :]))
        rows = np.arange(BLK)
        source = np.concatenate([rows, np.arange(-NEAR, 0), BLK + np.arange(NEAR)])
        down.append(pick(source[None, :] - rows[:, None]))
    return jnp.asarray(np.stack(across)), jnp.asarray(np.stack(down))


def box_sums(a):
    count = len(a) - 2 * EDGE
    two = {i: a[i] + a[i + 1] for i in range(4, 16)}
    three = {i: two[i] + a[i + 2] for i in range(6, 16)}
    four = {i: two[i] + two[i + 2] for i in range(4, 12)}
    own = four[7] + four[11]
    low = {6: a[6]}
    for i in range(5, -1, -1):
        low[i] = a[i] + low[i + 1]
    high = {1: a[15]}
    for i in range(2, 8):
        high[i] = high[i - 1] + a[i + 14]
    found = []
    for c in range(count):
        wide = own
        if c in low:
            wide = wide + low[c]
        if c in high:
            wide = wide + high[c]
        found.append((a[c + 7], three[c + 6], four[c + 4] + three[c + 8], wide))
    return found


def smooth_kernel(cpad_ref, across_ref, down_ref, out_ref, power_ref, acc_ref):
    k = pl.program_id(0)
    total = cpad_ref.shape[0]
    channels = total - 2 * EDGE

    def channel(c, _):
        across = jnp.dot(cpad_ref[c], across_ref[0], preferred_element_type=F32).astype(BF16)
        down = jnp.dot(down_ref[0], across, preferred_element_type=F32)
        out_ref[0, c] = down.astype(BF16)
        return 0

    lax.fori_loop(0, total, channel, 0)
    acc_ref[...] = jnp.zeros_like(acc_ref)

    def chunk(i, _):
        rows = pl.ds(pl.multiple_of((i // COLB) * NEAR, NEAR), NEAR)
        columns = pl.ds(pl.multiple_of((i % COLB) * BLK, BLK), BLK)
        a = [out_ref[0, c, rows, columns].astype(F32) for c in range(total)]
        for c, found in enumerate(box_sums(a)):
            for w, item in enumerate(found):
                square = item * item
                acc_ref[w, c] += square[:8] + square[8:]
        return 0

    lax.fori_loop(0, (BLK // NEAR) * COLB, chunk, 0)
    lane = lax.broadcasted_iota(jnp.int32, (channels, BLK), 1)

    @pl.when(k == 0)
    def _():
        power_ref[...] = jnp.zeros_like(power_ref)

    for w in range(WIDTHS):
        value = jnp.sum(jnp.sum(acc_ref[w], axis=1), axis=1, keepdims=True)
        power_ref[...] = jnp.where(lane == k * WIDTHS + w, value, power_ref[...])


def smooth_and_power(cpad):
    across, down = band_constants()
    total = cpad.shape[0]
    channels = total - 2 * EDGE
    return pl.pallas_call(
        smooth_kernel,
        grid=(KERNELS,),
        out_shape=(
            jax.ShapeDtypeStruct((KERNELS, total, BLK, COLB * BLK), BF16),
            jax.ShapeDtypeStruct((channels, BLK), F32),
        ),
        in_specs=[
            pl.BlockSpec(cpad.shape, lambda k: (0, 0, 0)),
            pl.BlockSpec((1,) + across.shape[1:], lambda k: (k, 0, 0)),
            pl.BlockSpec((1,) + down.shape[1:], lambda k: (k, 0, 0)),
        ],
        out_specs=(
            pl.BlockSpec((1, total, BLK, COLB * BLK), lambda k: (k, 0, 0, 0)),
            pl.BlockSpec((channels, BLK), lambda k: (0, 0)),
        ),
        scratch_shapes=[VMEM((WIDTHS, channels, 8, BLK), F32)],
        compiler_params=pltpu.CompilerParams(vmem_limit_bytes=40 * 2**20),
        name="smooth_and_power",
    )(cpad, across, down)


def factor_kernel(count, power_ref, clip_ref, factor_ref, arrived, send_sem, recv_sem):
    me = lax.axis_index("sky")
    barrier = pltpu.get_barrier_semaphore()

    def greet(d, _):
        pl.semaphore_signal(barrier, 1, device_id={"sky": lax.rem(me + d, count)}, device_id_type=MESH)
        return 0

    lax.fori_loop(1, count, greet, 0)
    pl.semaphore_wait(barrier, count - 1)

    def copy(d):
        return pltpu.make_async_remote_copy(
            src_ref=power_ref,
            dst_ref=arrived.at[d],
            send_sem=send_sem.at[d],
            recv_sem=recv_sem.at[d],
            device_id={"sky": lax.rem(me + d, count)},
            device_id_type=MESH,
        )

    def start(d, _):
        copy(d).start()
        return 0

    def finish(d, _):
        copy(d).wait()
        return 0

    lax.fori_loop(1, count, start, 0)
    lax.fori_loop(1, count, finish, 0)
    total = power_ref[...]
    for d in range(1, count):
        total = total + arrived[d]
    noise = jnp.sqrt(total * (1.0 / CELLS) + EPSILON)
    factor_ref[...] = 10.0 / (clip_ref[...] * noise)


def clip_factors(power, clip_tenths):
    channels = power.shape[0]
    clip = clip_tenths.astype(F32).reshape(1, KERNELS * WIDTHS)
    clip = jnp.pad(clip, ((0, 0), (0, BLK - KERNELS * WIDTHS)), constant_values=1.0)
    clip = jnp.broadcast_to(clip, (channels, BLK))
    count = lax.axis_size("sky")
    return pl.pallas_call(
        functools.partial(factor_kernel, count),
        out_shape=jax.ShapeDtypeStruct(power.shape, F32),
        in_specs=[pl.BlockSpec(memory_space=VMEM)] * 2,
        out_specs=pl.BlockSpec(memory_space=VMEM),
        scratch_shapes=[
            VMEM((count, channels, BLK), F32),
            pltpu.SemaphoreType.DMA((count,)),
            pltpu.SemaphoreType.DMA((count,)),
        ],
        compiler_params=pltpu.CompilerParams(collective_id=3, has_side_effects=True),
        name="clip_factors",
    )(power, clip)


def score_kernel(factor_ref, smoothed_ref, out_ref):
    total = smoothed_ref.shape[1]
    for column in range(COLB):
        columns = slice(column * BLK, (column + 1) * BLK)
        best = [None] * (total - 2 * EDGE)
        for k in range(KERNELS):
            a = [smoothed_ref[k, c, :, columns].astype(F32) for c in range(total)]
            for c, found in enumerate(box_sums(a)):
                for w, item in enumerate(found):
                    score = jnp.abs(item) * factor_ref[c, k * WIDTHS + w]
                    best[c] = score if best[c] is None else jnp.maximum(best[c], score)
        for c, item in enumerate(best):
            out_ref[c, :, columns] = item


def scores(factor, smoothed):
    total = smoothed.shape[1]
    channels = total - 2 * EDGE
    return pl.pallas_call(
        score_kernel,
        grid=(BLK // NEAR,),
        out_shape=jax.ShapeDtypeStruct((channels, BLK, COLB * BLK), F32),
        in_specs=[
            pl.BlockSpec(memory_space=pltpu.SMEM),
            pl.BlockSpec((KERNELS, total, NEAR, COLB * BLK), lambda i: (0, 0, i, 0)),
        ],
        out_specs=pl.BlockSpec((channels, NEAR, COLB * BLK), lambda i: (0, i, 0)),
        compiler_params=pltpu.CompilerParams(vmem_limit_bytes=40 * 2**20),
        name="scores",
    )(factor, smoothed)


def neighbours(axis):
    count = lax.axis_size(axis)
    forward = [(i, i + 1) for i in range(count - 1)]
    backward = [(target, source) for source, target in forward]
    return forward, backward


def owner_tables(beams_in, labels_in, tile_blocks):
    onehot = labels_in[None, :] == jnp.arange(tile_blocks)[:, None]
    beam_wide = beams_in.astype(F32)
    coverage = (
        jnp.einsum(
            "bs,syx->byx", onehot.astype(F32), beam_wide * beam_wide, precision=lax.Precision.HIGHEST
        )
        + REGULARIZER
    )
    return (onehot.astype(BF16), coverage)


def block_values(onehot, coverage, arrived):
    numerator = jnp.einsum("bs,scyx->bcyx", onehot, arrived, preferred_element_type=F32)
    return (numerator / coverage[:, None]).astype(BF16)


def shards(pieces, beam, destination, clip_tenths):
    sky_count = lax.axis_size("sky")
    piece_count, channels, block_size, _ = pieces.shape
    tile_blocks = ROWB * COLB
    capacity = max(2, 2 * piece_count // sky_count)
    slot_total = sky_count * capacity
    owners = destination // tile_blocks
    numbering = jnp.arange(piece_count)
    earlier = (owners[None, :] == owners[:, None]) & (numbering[None, :] < numbering[:, None])
    position = jnp.sum(earlier.astype(jnp.int32), axis=1)
    slot_index = owners * capacity + position
    weighted = (beam[:, None].astype(F32) * pieces.astype(F32)).astype(BF16)
    outgoing = jnp.zeros((slot_total, channels, block_size, block_size), BF16).at[slot_index].set(weighted)
    beams_out = jnp.zeros((slot_total, block_size, block_size), BF16).at[slot_index].set(beam)
    labels_out = jnp.full((slot_total,), -1, jnp.int32).at[slot_index].set(destination % tile_blocks)
    arrived, beams_in, labels_in = (
        lax.all_to_all(outgoing, "sky", split_axis=0, concat_axis=0, tiled=True),
        lax.all_to_all(beams_out, "sky", split_axis=0, concat_axis=0, tiled=True),
        lax.all_to_all(labels_out, "sky", split_axis=0, concat_axis=0, tiled=True),
    )
    onehot, coverage = owner_tables(beams_in, labels_in, tile_blocks)
    tile_values = block_values(onehot, coverage, arrived)
    combined = tile_values.reshape(ROWB, COLB, channels, block_size, block_size).transpose(2, 0, 3, 1, 4)
    combined = combined.reshape(channels, ROWB * block_size, COLB * block_size)
    forward, backward = neighbours("sky")
    above = lax.ppermute(combined[:, -NEAR:], "sky", forward)
    below = lax.ppermute(combined[:, :NEAR], "sky", backward)
    tall = jnp.concatenate([combined, above, below], axis=1)
    forward, backward = neighbours("freq")
    low = lax.ppermute(tall[-EDGE:], "freq", forward)
    high = lax.ppermute(tall[:EDGE], "freq", backward)
    cpad = jnp.concatenate([low, tall, high], axis=0)
    smoothed, power = smooth_and_power(cpad)
    factor = clip_factors(power, clip_tenths)
    return scores(factor, smoothed)


def solution(mesh):
    return jax.shard_map(
        shards,
        mesh=mesh,
        in_specs=(P("sky", "freq", None, None), P("sky", None, None), P("sky"), P()),
        out_specs=P("freq", "sky", None),
        check_vma=False,
    )
```

```python
import functools
import numpy as np
import ml_dtypes
import jax
import jax.numpy as jnp
from jax import lax
from jax.experimental import pallas as pl
from jax.experimental.pallas import tpu as pltpu
from jax.sharding import PartitionSpec as P

ROWB = 1
COLB = 4
BLK = 128
RIM = 8
EDGE = 7
KERNELS = 3
WIDTHS = 4
NEAR = 16
REGULARIZER = 0.05
EPSILON = 1e-06
KERNEL_FWHM = (3.0, 6.0, 9.0)
HALF_WIDTHS = (0, 1, 3, 7)
CELLS = 2048 * 512
MESH = pl.DeviceIdType.MESH
VMEM = pltpu.VMEM
F32 = jnp.float32
BF16 = jnp.bfloat16


def band_constants():
    across, down = [], []
    for fwhm in KERNEL_FWHM:
        offsets = np.arange(-RIM, RIM + 1).astype(np.float32)
        sigma = np.float32(fwhm / 2.3548)
        taps = np.exp(-offsets * offsets / (np.float32(2.0) * sigma * sigma)).astype(ml_dtypes.bfloat16)

        def pick(distance):
            inside = np.abs(distance) <= RIM
            return np.where(inside, taps[np.clip(distance + RIM, 0, 2 * RIM)], taps.dtype.type(0))

        columns = np.arange(COLB * BLK)
        across.append(pick(columns[:, None] - columns[None, :]))
        rows = np.arange(BLK)
        source = np.concatenate([rows, np.arange(-NEAR, 0), BLK + np.arange(NEAR)])
        down.append(pick(source[None, :] - rows[:, None]))
    return jnp.asarray(np.stack(across)), jnp.asarray(np.stack(down))


def box_sums(a):
    count = len(a) - 2 * EDGE
    two = {i: a[i] + a[i + 1] for i in range(4, 16)}
    three = {i: two[i] + a[i + 2] for i in range(6, 16)}
    four = {i: two[i] + two[i + 2] for i in range(4, 12)}
    own = four[7] + four[11]
    low = {6: a[6]}
    for i in range(5, -1, -1):
        low[i] = a[i] + low[i + 1]
    high = {1: a[15]}
    for i in range(2, 8):
        high[i] = high[i - 1] + a[i + 14]
    found = []
    for c in range(count):
        wide = own
        if c in low:
            wide = wide + low[c]
        if c in high:
            wide = wide + high[c]
        found.append((a[c + 7], three[c + 6], four[c + 4] + three[c + 8], wide))
    return found


def smooth_kernel(cpad_ref, across_ref, down_ref, out_ref, power_ref, acc_ref):
    k = pl.program_id(0)
    total = cpad_ref.shape[0] - 2
    channels = total - 2 * EDGE

    def channel(c, _):
        across = jnp.dot(cpad_ref[c + 1], across_ref[0], preferred_element_type=F32).astype(BF16)
        down = jnp.dot(down_ref[0], across, preferred_element_type=F32)
        out_ref[0, c] = down.astype(BF16)
        return 0

    lax.fori_loop(0, total, channel, 0)
    acc_ref[...] = jnp.zeros_like(acc_ref)

    def chunk(i, _):
        rows = pl.ds(pl.multiple_of((i // COLB) * NEAR, NEAR), NEAR)
        columns = pl.ds(pl.multiple_of((i % COLB) * BLK, BLK), BLK)
        a = [out_ref[0, c, rows, columns].astype(F32) for c in range(total)]
        for c, found in enumerate(box_sums(a)):
            for w, item in enumerate(found):
                square = item * item
                acc_ref[w, c] += square[:8] + square[8:]
        return 0

    lax.fori_loop(0, (BLK // NEAR) * COLB, chunk, 0)
    lane = lax.broadcasted_iota(jnp.int32, (channels, BLK), 1)

    @pl.when(k == 0)
    def _():
        power_ref[...] = jnp.zeros_like(power_ref)

    for w in range(WIDTHS):
        value = jnp.sum(jnp.sum(acc_ref[w], axis=1), axis=1, keepdims=True)
        power_ref[...] = jnp.where(lane == k * WIDTHS + w, value, power_ref[...])


def smooth_and_power(cpad):
    across, down = band_constants()
    total = cpad.shape[0] - 2
    channels = total - 2 * EDGE
    return pl.pallas_call(
        smooth_kernel,
        grid=(KERNELS,),
        out_shape=(
            jax.ShapeDtypeStruct((KERNELS, total, BLK, COLB * BLK), BF16),
            jax.ShapeDtypeStruct((channels, BLK), F32),
        ),
        in_specs=[
            pl.BlockSpec(cpad.shape, lambda k: (0, 0, 0)),
            pl.BlockSpec((1,) + across.shape[1:], lambda k: (k, 0, 0)),
            pl.BlockSpec((1,) + down.shape[1:], lambda k: (k, 0, 0)),
        ],
        out_specs=(
            pl.BlockSpec((1, total, BLK, COLB * BLK), lambda k: (k, 0, 0, 0)),
            pl.BlockSpec((channels, BLK), lambda k: (0, 0)),
        ),
        scratch_shapes=[VMEM((WIDTHS, channels, 8, BLK), F32)],
        compiler_params=pltpu.CompilerParams(vmem_limit_bytes=40 * 2**20),
        name="smooth_and_power",
    )(cpad, across, down)


def factor_kernel(count, power_ref, clip_ref, factor_ref, arrived, send_sem, recv_sem):
    me = lax.axis_index("sky")
    barrier = pltpu.get_barrier_semaphore()

    def greet(d, _):
        pl.semaphore_signal(barrier, 1, device_id={"sky": lax.rem(me + d, count)}, device_id_type=MESH)
        return 0

    lax.fori_loop(1, count, greet, 0)
    pl.semaphore_wait(barrier, count - 1)

    def copy(d):
        return pltpu.make_async_remote_copy(
            src_ref=power_ref,
            dst_ref=arrived.at[d],
            send_sem=send_sem.at[d],
            recv_sem=recv_sem.at[d],
            device_id={"sky": lax.rem(me + d, count)},
            device_id_type=MESH,
        )

    def start(d, _):
        copy(d).start()
        return 0

    def finish(d, _):
        copy(d).wait()
        return 0

    lax.fori_loop(1, count, start, 0)
    lax.fori_loop(1, count, finish, 0)
    total = power_ref[...]
    for d in range(1, count):
        total = total + arrived[d]
    noise = jnp.sqrt(total * (1.0 / CELLS) + EPSILON)
    factor_ref[...] = 10.0 / (clip_ref[...] * noise)


def clip_factors(power, clip_tenths):
    channels = power.shape[0]
    clip = clip_tenths.astype(F32).reshape(1, KERNELS * WIDTHS)
    clip = jnp.pad(clip, ((0, 0), (0, BLK - KERNELS * WIDTHS)), constant_values=1.0)
    clip = jnp.broadcast_to(clip, (channels, BLK))
    count = lax.axis_size("sky")
    return pl.pallas_call(
        functools.partial(factor_kernel, count),
        out_shape=jax.ShapeDtypeStruct(power.shape, F32),
        in_specs=[pl.BlockSpec(memory_space=VMEM)] * 2,
        out_specs=pl.BlockSpec(memory_space=VMEM),
        scratch_shapes=[
            VMEM((count, channels, BLK), F32),
            pltpu.SemaphoreType.DMA((count,)),
            pltpu.SemaphoreType.DMA((count,)),
        ],
        compiler_params=pltpu.CompilerParams(collective_id=3, has_side_effects=True),
        name="clip_factors",
    )(power, clip)


def score_kernel(factor_ref, smoothed_ref, out_ref):
    total = smoothed_ref.shape[1]
    for column in range(COLB):
        columns = slice(column * BLK, (column + 1) * BLK)
        best = [None] * (total - 2 * EDGE)
        for k in range(KERNELS):
            a = [smoothed_ref[k, c, :, columns].astype(F32) for c in range(total)]
            for c, found in enumerate(box_sums(a)):
                for w, item in enumerate(found):
                    score = jnp.abs(item) * factor_ref[c, k * WIDTHS + w]
                    best[c] = score if best[c] is None else jnp.maximum(best[c], score)
        for c, item in enumerate(best):
            out_ref[c, :, columns] = item


def scores(factor, smoothed):
    total = smoothed.shape[1]
    channels = total - 2 * EDGE
    return pl.pallas_call(
        score_kernel,
        grid=(BLK // NEAR,),
        out_shape=jax.ShapeDtypeStruct((channels, BLK, COLB * BLK), F32),
        in_specs=[
            pl.BlockSpec(memory_space=pltpu.SMEM),
            pl.BlockSpec((KERNELS, total, NEAR, COLB * BLK), lambda i: (0, 0, i, 0)),
        ],
        out_specs=pl.BlockSpec((channels, NEAR, COLB * BLK), lambda i: (0, i, 0)),
        compiler_params=pltpu.CompilerParams(vmem_limit_bytes=40 * 2**20),
        name="scores",
    )(factor, smoothed)


SIDE = 4
GROUP = 4
PIECES = 8
STEPS = ((0, 1), (0, -1), (1, 0), (-1, 0), (1, 1), (1, -1), (-1, 1), (-1, -1))
HALF = COLB // 2


def combine_kernel(
    sky_count, freq_count, pieces_ref, beam_ref, label_ref, cpad_ref,
    held, first_out, first_in, second_out, second_in, label_all, label_s,
    cover_out, cover_in, inverse,
    label_sems, label_local, cover_sems, inverse_sems, wave_sems, hop_sems, first_sems, second_sems,
    edge_send, edge_recv,
):
    t, f = lax.axis_index("sky"), lax.axis_index("freq")
    x, y = t // SIDE, lax.rem(t, SIDE)
    barrier = pltpu.get_barrier_semaphore()

    def at(o, d):
        if o == 0:
            return lax.rem(x + d + SIDE, SIDE) * SIDE + y
        return x * SIDE + lax.rem(y + d + SIDE, SIDE)

    def remote(source, target, send, recv, sky, freq):
        return pltpu.make_async_remote_copy(
            src_ref=source, dst_ref=target, send_sem=send, recv_sem=recv,
            device_id=(sky, freq), device_id_type=MESH,
        )

    def within(dt, df):
        good = None
        for value, delta, count in ((t, dt, sky_count), (f, df, freq_count)):
            if delta:
                here = value + delta
                one = (here >= 0) & (here < count)
                good = one if good is None else good & one
        return good

    def greet_sky(d, _):
        pl.semaphore_signal(barrier, 1, device_id=(lax.rem(t + d, sky_count), f), device_id_type=MESH)
        return 0

    def greet_freq(d, _):
        pl.semaphore_signal(barrier, 1, device_id=(t, lax.rem(f + d, freq_count)), device_id_type=MESH)
        return 0

    lax.fori_loop(1, sky_count, greet_sky, 0)
    lax.fori_loop(1, freq_count, greet_freq, 0)
    for dt, df in STEPS[4:]:
        @pl.when(within(dt, df))
        def _():
            pl.semaphore_signal(barrier, 1, device_id=(t + dt, f + df), device_id_type=MESH)

    def weigh(c, _):
        for p in range(PIECES):
            value = beam_ref[p].astype(F32) * pieces_ref[p, c].astype(F32)
            held[c, 0, p] = value.astype(BF16)
        return 0

    lax.fori_loop(0, 2 * GROUP, weigh, 0)

    total = cpad_ref.shape[0]
    for edge, rows in ((t == 0, pl.ds(BLK, NEAR)), (t == sky_count - 1, pl.ds(BLK + NEAR, NEAR))):
        @pl.when(edge)
        def _():
            def clear(c, _):
                cpad_ref[c, rows, :] = jnp.zeros((NEAR, COLB * BLK), BF16)
                return 0
            lax.fori_loop(0, total, clear, 0)
    for edge, start in ((f == 0, 0), (f == freq_count - 1, 4 * GROUP)):
        @pl.when(edge)
        def _():
            def clear(c, _):
                cpad_ref[start + c] = jnp.zeros(cpad_ref.shape[1:], BF16)
                return 0
            lax.fori_loop(0, 2 * GROUP, clear, 0)

    diagonals = jnp.int32(0)
    for dt, df in STEPS[4:]:
        diagonals = diagonals + within(dt, df).astype(jnp.int32)
    pl.semaphore_wait(barrier, sky_count - 1 + freq_count - 1 + diagonals)

    def wave(o, i, side):
        c = o * GROUP + i
        return remote(
            held.at[c, 0], held.at[c, 1 if side == 1 else 3],
            wave_sems.at[0, c, (1 - side) // 2], wave_sems.at[1, c, (1 - side) // 2], at(o, side), f,
        )

    def onward(o, i, side):
        c = o * GROUP + i
        half = pl.ds(0 if side == 1 else PIECES // 2, PIECES // 2)
        return remote(
            held.at[c, 1 if side == 1 else 3, half], held.at[c, 2, half],
            hop_sems.at[0, c, (1 - side) // 2], hop_sems.at[1, c, (1 - side) // 2], at(o, side), f,
        )

    def first(o, i, side):
        c = o * GROUP + i
        n = (1 - side) // 2
        return remote(
            first_out.at[c, n], first_in.at[c, n], first_sems.at[0, c, n], first_sems.at[1, c, n], at(1 - o, side), f
        )

    def second(o, i, side):
        c = o * GROUP + i
        n = (1 - side) // 2
        return remote(
            second_out.at[c, n], second_in.at[c, n], second_sems.at[0, c, n], second_sems.at[1, c, n],
            at(1 - o, side), f,
        )

    SIDES = (1, -1)
    ORIENTATIONS = (0, 1)

    def label_copy(d):
        return remote(
            label_ref, label_all.at[t], label_sems.at[0, d], label_sems.at[1, d], lax.rem(t + d, sky_count), f
        )

    def start_labels(d, _):
        label_copy(d).start()
        return 0

    lax.fori_loop(1, sky_count, start_labels, 0)
    for o in ORIENTATIONS:
        for side in SIDES:
            wave(o, 0, side).start()

    pair = pl.ds(pl.multiple_of((f // 2) * NEAR, NEAR), NEAR)
    squares = []
    for p in range(PIECES):
        both = beam_ref[p, pair, :].astype(F32)
        mine = jnp.where(lax.rem(f, 2) == 0, both[:8], both[8:])
        squares.append(mine * mine)
    labels = [jnp.broadcast_to(label_ref[p : p + 1, :], (8, BLK)) for p in range(PIECES)]

    def cover(tile, _):
        for b in range(COLB):
            found = jnp.zeros((8, BLK), F32)
            for p in range(PIECES):
                found = found + jnp.where(labels[p] == tile * COLB + b, squares[p], 0.0)
            cover_out[tile, b] = found
        return 0

    lax.fori_loop(0, sky_count, cover, 0)

    def cover_copy(d):
        other = lax.rem(t + d, sky_count)
        return remote(cover_out.at[other], cover_in.at[d], cover_sems.at[0, d], cover_sems.at[1, d], other, f)

    def start_cover(d, _):
        cover_copy(d).start()
        return 0

    lax.fori_loop(1, sky_count, start_cover, 0)
    for o in ORIENTATIONS:
        for side in SIDES:
            wave(o, 1, side).start()

    def finish_labels(d, _):
        label_copy(d).wait_send()
        source = lax.rem(t - d + sky_count, sky_count)
        remote(
            label_ref, label_all.at[source], label_sems.at[0, d], label_sems.at[1, d], source, f
        ).wait_recv()
        return 0

    label_all[t] = label_ref[...]
    lax.fori_loop(1, sky_count, finish_labels, 0)
    to_scalars = pltpu.make_async_copy(label_all, label_s, label_local)
    to_scalars.start()

    def finish_cover(d, _):
        cover_copy(d).wait()
        return 0

    lax.fori_loop(1, sky_count, finish_cover, 0)
    coverage = cover_out[t] + REGULARIZER
    for d in range(1, sky_count):
        coverage = coverage + cover_in[d]
    inverse[f] = 1.0 / coverage

    def inverse_copy(d):
        return remote(
            inverse.at[f], inverse.at[f], inverse_sems.at[0, d], inverse_sems.at[1, d],
            t, lax.rem(f + d, freq_count),
        )

    def start_inverse(d, _):
        inverse_copy(d).start()
        return 0

    lax.fori_loop(1, freq_count, start_inverse, 0)
    to_scalars.wait()

    def finish_inverse(d, _):
        inverse_copy(d).wait_send()
        source = lax.rem(f - d + freq_count, freq_count)
        remote(
            inverse.at[source], inverse.at[source], inverse_sems.at[0, d], inverse_sems.at[1, d], t, source
        ).wait_recv()
        return 0

    ROWS = 64

    def sums(o, c, d, blocks, rows):
        base = at(1 - o, d) * COLB

        def source(j, found):
            sky = at(o, -j)
            found = list(found)
            for p in range(PIECES):
                value = held[c, j, p, rows, :].astype(F32)
                label = label_s[sky, p, 0]
                for n, b in enumerate(blocks):
                    found[n] = found[n] + jnp.where(label == base + b, 1.0, 0.0) * value
            return tuple(found)

        return lax.fori_loop(0, SIDE, source, tuple(jnp.zeros((ROWS, BLK), F32) for _ in blocks))

    def by_rows(body):
        def chunk(r, _):
            body(pl.ds(pl.multiple_of(r * ROWS, ROWS), ROWS), r)
            return 0
        lax.fori_loop(0, BLK // ROWS, chunk, 0)

    def edge_copy(c, n):
        dt, df = STEPS[n]
        rows = {0: pl.ds(0, BLK), 1: pl.ds(BLK - NEAR, NEAR), -1: pl.ds(0, NEAR)}[dt]
        land = {0: pl.ds(0, BLK), 1: pl.ds(BLK, NEAR), -1: pl.ds(BLK + NEAR, NEAR)}[dt]
        own = 2 * GROUP + c
        return remote(
            cpad_ref.at[own, rows], cpad_ref.at[own - 2 * GROUP * df, land],
            edge_send.at[n, c], edge_recv.at[n, c], t + dt, f + df,
        )

    def step(n, _):
        @pl.when(n < GROUP)
        def _():
            for o in ORIENTATIONS:
                for side in SIDES:
                    wave(o, n, side).wait_recv()
                    onward(o, n, side).start()

        @pl.when(n < GROUP - 2)
        def _():
            for o in ORIENTATIONS:
                for side in SIDES:
                    wave(o, n + 2, side).start()

        @pl.when((n >= 1) & (n < GROUP + 1))
        def _():
            i = n - 1
            for o in ORIENTATIONS:
                c = o * GROUP + i
                for side in SIDES:
                    onward(o, i, side).wait_recv()

                def far(rows, r):
                    found = sums(o, c, 2, tuple(range(COLB)), rows)
                    for b in range(COLB):
                        first_out[c, b // HALF, b % HALF, rows, :] = found[b].astype(BF16)

                by_rows(far)
                for side in SIDES:
                    first(o, i, side).start()

        @pl.when((n >= 2) & (n < GROUP + 2))
        def _():
            i = n - 2
            for o in ORIENTATIONS:
                c = o * GROUP + i
                for m, side in enumerate(SIDES):
                    first(o, i, side).wait_recv()

                    def near(rows, r):
                        found = list(sums(o, c, side, tuple(range(COLB)), rows))
                        for b in range(HALF):
                            found[m * HALF + b] = found[m * HALF + b] + first_in[c, m, b, rows, :].astype(F32)
                        for b in range(COLB):
                            second_out[c, m, b, rows, :] = found[b].astype(BF16)

                    by_rows(near)
                    second(o, i, side).start()

        @pl.when(n == 3)
        def _():
            lax.fori_loop(1, freq_count, finish_inverse, 0)

        @pl.when(n >= 3)
        def _():
            i = n - 3
            for o in ORIENTATIONS:
                c = o * GROUP + i
                for side in SIDES:
                    second(o, i, side).wait_recv()

                def own(rows, r):
                    found = sums(o, c, 0, tuple(range(COLB)), rows)
                    for b in range(COLB):
                        value = found[b]
                        for m in range(2):
                            value = value + second_in[c, m, b, rows, :].astype(F32)
                        scale = jnp.concatenate([inverse[r * (ROWS // 8) + q, b] for q in range(ROWS // 8)], axis=0)
                        cpad_ref[2 * GROUP + c, rows, b * BLK : (b + 1) * BLK] = (value * scale).astype(BF16)

                by_rows(own)
                for m, (dt, df) in enumerate(STEPS):
                    @pl.when(within(dt, df))
                    def _():
                        edge_copy(c, m).start()
        return 0

    lax.fori_loop(0, GROUP + 3, step, 0)

    def finish(c, _):
        for m, (dt, df) in enumerate(STEPS):
            @pl.when(within(-dt, -df))
            def _():
                edge_copy(c, m).wait_recv()

            @pl.when(within(dt, df))
            def _():
                edge_copy(c, m).wait_send()
        return 0

    lax.fori_loop(0, 2 * GROUP, finish, 0)

    def drain(i, _):
        for o in ORIENTATIONS:
            for side in SIDES:
                for copy in (wave, onward, first, second):
                    copy(o, i, side).wait_send()
        return 0

    lax.fori_loop(0, GROUP, drain, 0)


def combine(pieces, beam, destination):
    sky_count, freq_count = lax.axis_size("sky"), lax.axis_size("freq")
    piece_count, channels = pieces.shape[:2]
    labels = jnp.broadcast_to(destination[:, None], (piece_count, BLK))
    dma = pltpu.SemaphoreType.DMA
    plane = (BLK, BLK)
    return pl.pallas_call(
        functools.partial(combine_kernel, sky_count, freq_count),
        out_shape=jax.ShapeDtypeStruct((3 * channels, BLK + 2 * NEAR, COLB * BLK), BF16),
        in_specs=[pl.BlockSpec(memory_space=VMEM)] * 3,
        out_specs=pl.BlockSpec(memory_space=VMEM),
        scratch_shapes=[
            VMEM((channels, SIDE, piece_count) + plane, BF16),
            VMEM((channels, 2, HALF) + plane, BF16),
            VMEM((channels, 2, HALF) + plane, BF16),
            VMEM((channels, 2, COLB) + plane, BF16),
            VMEM((channels, 2, COLB) + plane, BF16),
            VMEM((sky_count, piece_count, BLK), jnp.int32),
            pltpu.SMEM((sky_count, piece_count, BLK), jnp.int32),
            VMEM((sky_count, COLB, 8, BLK), F32),
            VMEM((sky_count, COLB, 8, BLK), F32),
            VMEM((freq_count, COLB, 8, BLK), F32),
            dma((2, sky_count)),
            dma,
            dma((2, sky_count)),
            dma((2, freq_count)),
            dma((2, channels, 2)),
            dma((2, channels, 2)),
            dma((2, channels, 2)),
            dma((2, channels, 2)),
            dma((len(STEPS), channels)),
            dma((len(STEPS), channels)),
        ],
        compiler_params=pltpu.CompilerParams(
            collective_id=1, has_side_effects=True, vmem_limit_bytes=48 * 2**20
        ),
        name="combine",
    )(pieces, beam, labels)


def shards(pieces, beam, destination, clip_tenths):
    cpad = combine(pieces, beam, destination)
    smoothed, power = smooth_and_power(cpad)
    factor = clip_factors(power, clip_tenths)
    return scores(factor, smoothed)


def solution(mesh):
    return jax.shard_map(
        shards,
        mesh=mesh,
        in_specs=(P("sky", "freq", None, None), P("sky", None, None), P("sky"), P()),
        out_specs=P("freq", "sky", None),
        check_vma=False,
    )
```

```python
import functools
import numpy as np
import ml_dtypes
import jax
import jax.numpy as jnp
from jax import lax
from jax.experimental import pallas as pl
from jax.experimental.pallas import tpu as pltpu
from jax.sharding import PartitionSpec as P

ROWB = 1
COLB = 4
BLK = 128
RIM = 8
EDGE = 7
KERNELS = 3
WIDTHS = 4
NEAR = 16
REGULARIZER = 0.05
EPSILON = 1e-06
KERNEL_FWHM = (3.0, 6.0, 9.0)
HALF_WIDTHS = (0, 1, 3, 7)
CELLS = 2048 * 512
WINDOW = 256
MESH = pl.DeviceIdType.MESH
VMEM = pltpu.VMEM
F32 = jnp.float32
BF16 = jnp.bfloat16


def band_constants():
    across, down = [], [[], []]
    for fwhm in KERNEL_FWHM:
        offsets = np.arange(-RIM, RIM + 1).astype(np.float32)
        sigma = np.float32(fwhm / 2.3548)
        taps = np.exp(-offsets * offsets / (np.float32(2.0) * sigma * sigma)).astype(ml_dtypes.bfloat16)

        def pick(distance):
            inside = np.abs(distance) <= RIM
            return np.where(inside, taps[np.clip(distance + RIM, 0, 2 * RIM)], taps.dtype.type(0))

        columns = np.arange(WINDOW)
        across.append(pick(columns[:, None] - columns[None, :]))
        rows = np.arange(BLK)
        away = np.full(RIM, 4 * BLK)
        above, below = np.arange(-RIM, 0), BLK + np.arange(RIM)
        for half, order in enumerate((lambda v: [v, away], lambda v: [away, v])):
            source = np.concatenate([rows] + order(above) + order(below))
            down[half].append(pick(source[None, :] - rows[:, None]))
    return jnp.asarray(np.stack(across)), jnp.asarray(np.stack([np.concatenate(half) for half in down]))


def box_sums(a):
    count = len(a) - 2 * EDGE
    two = {i: a[i] + a[i + 1] for i in range(4, 16)}
    three = {i: two[i] + a[i + 2] for i in range(6, 16)}
    four = {i: two[i] + two[i + 2] for i in range(4, 12)}
    own = four[7] + four[11]
    low = {6: a[6]}
    for i in range(5, -1, -1):
        low[i] = a[i] + low[i + 1]
    high = {1: a[15]}
    for i in range(2, 8):
        high[i] = high[i - 1] + a[i + 14]
    found = []
    for c in range(count):
        wide = own
        if c in low:
            wide = wide + low[c]
        if c in high:
            wide = wide + high[c]
        found.append((a[c + 7], three[c + 6], four[c + 4] + three[c + 8], wide))
    return found


SIDE = 4
GROUP = 4
PIECES = 8
DIAGONALS = ((1, 1), (1, -1), (-1, 1), (-1, -1))
EDGES = ((1, 0), (-1, 0)) + DIAGONALS
HALF = COLB // 2
ROWS = 64
SIDES = (1, -1)
ORIENTATIONS = (0, 1)


def whole_kernel(
    sky_count, freq_count, pieces_hbm, beam_hbm, destination_ref, clip_ref, across_ref, down_ref, out_ref,
    pieces_ref, beam_ref, label_ref, held, first_out, first_in, second_out, second_in, label_all, label_s,
    cover_out, cover_in, inverse, main, edge_out, edge_in, halfway, smoothed, acc, power_out, power_in, factor_v,
    factor_s,
    load_sems, label_sems, local_sems, cover_sems, inverse_sems, wave_sems, hop_sems, first_sems, second_sems,
    main_sems, edge_sems, power_sems,
):
    t, f = lax.axis_index("sky"), lax.axis_index("freq")
    x, y = t // SIDE, lax.rem(t, SIDE)
    load_pieces = pltpu.make_async_copy(pieces_hbm, pieces_ref, load_sems.at[0])
    load_beam = pltpu.make_async_copy(beam_hbm, beam_ref, load_sems.at[1])
    load_beam.start()
    load_pieces.start()
    barrier = pltpu.get_barrier_semaphore()

    def at(o, d):
        if o == 0:
            return lax.rem(x + d + SIDE, SIDE) * SIDE + y
        return x * SIDE + lax.rem(y + d + SIDE, SIDE)

    def remote(source, target, sems, where, sky, freq):
        return pltpu.make_async_remote_copy(
            src_ref=source, dst_ref=target, send_sem=sems.at[(0,) + where], recv_sem=sems.at[(1,) + where],
            device_id=(sky, freq), device_id_type=MESH,
        )

    def within(dt, df):
        good = None
        for value, delta, count in ((t, dt, sky_count), (f, df, freq_count)):
            if delta:
                here = value + delta
                one = (here >= 0) & (here < count)
                good = one if good is None else good & one
        return good

    def greet_sky(d, _):
        pl.semaphore_signal(barrier, 1, device_id=(lax.rem(t + d, sky_count), f), device_id_type=MESH)
        return 0

    def greet_freq(d, _):
        pl.semaphore_signal(barrier, 1, device_id=(t, lax.rem(f + d, freq_count)), device_id_type=MESH)
        return 0

    lax.fori_loop(1, sky_count, greet_sky, 0)
    lax.fori_loop(1, freq_count, greet_freq, 0)
    for dt, df in DIAGONALS:
        @pl.when(within(dt, df))
        def _():
            pl.semaphore_signal(barrier, 1, device_id=(t + dt, f + df), device_id_type=MESH)

    for p in range(PIECES):
        label_ref[p : p + 1, :] = jnp.full((1, BLK), destination_ref[p], jnp.int32)
    label_all[t] = label_ref[...]

    for edge, n in ((t == 0, 0), (t == sky_count - 1, 1)):
        @pl.when(edge)
        def _():
            for g in range(3):
                for i in range(GROUP):
                    edge_in[g, i, n] = jnp.zeros((NEAR, COLB * BLK), BF16)
    for edge, g in ((f == 0, 0), (f == freq_count - 1, 2)):
        @pl.when(edge)
        def _():
            edge_in[g] = jnp.zeros(edge_in.shape[1:], BF16)

            def clear(c, _):
                main[g * 2 * GROUP + c] = jnp.zeros(main.shape[1:], BF16)
                return 0

            lax.fori_loop(0, 2 * GROUP, clear, 0)

    load_beam.wait()
    load_pieces.wait()

    def weigh(c, _):
        for p in range(PIECES):
            value = beam_ref[p].astype(F32) * pieces_ref[p, c].astype(F32)
            held[c, 0, p] = value.astype(BF16)
        return 0

    lax.fori_loop(0, 2 * GROUP, weigh, 0)
    diagonals = jnp.int32(0)
    for dt, df in DIAGONALS:
        diagonals = diagonals + within(dt, df).astype(jnp.int32)
    pl.semaphore_wait(barrier, sky_count - 1 + freq_count - 1 + diagonals)

    def wave(o, i, side):
        c = o * GROUP + i
        n = (1 - side) // 2
        return remote(held.at[c, 0], held.at[c, 1 if side == 1 else 3], wave_sems, (c, n), at(o, side), f)

    def onward(o, i, side):
        c = o * GROUP + i
        n = (1 - side) // 2
        half = pl.ds(n * (PIECES // 2), PIECES // 2)
        return remote(
            held.at[c, 1 if side == 1 else 3, half], held.at[c, 2, half], hop_sems, (c, n), at(o, side), f
        )

    def first(o, i, side):
        c = o * GROUP + i
        n = (1 - side) // 2
        return remote(first_out.at[c, n], first_in.at[c, n], first_sems, (c, n), at(1 - o, side), f)

    def second(o, i, side):
        c = o * GROUP + i
        n = (1 - side) // 2
        return remote(second_out.at[c, n], second_in.at[c, n], second_sems, (c, n), at(1 - o, side), f)

    def label_copy(d):
        return remote(label_ref, label_all.at[t], label_sems, (d,), lax.rem(t + d, sky_count), f)

    def start_labels(d, _):
        label_copy(d).start()
        return 0

    lax.fori_loop(1, sky_count, start_labels, 0)
    for o in ORIENTATIONS:
        for side in SIDES:
            wave(o, 0, side).start()

    pair = pl.ds(pl.multiple_of((f // 2) * NEAR, NEAR), NEAR)
    squares = []
    for p in range(PIECES):
        both = beam_ref[p, pair, :].astype(F32)
        mine = jnp.where(lax.rem(f, 2) == 0, both[:8], both[8:])
        squares.append(mine * mine)
    labels = [jnp.broadcast_to(label_ref[p : p + 1, :], (8, BLK)) for p in range(PIECES)]

    def cover(tile, _):
        for b in range(COLB):
            found = jnp.zeros((8, BLK), F32)
            for p in range(PIECES):
                found = found + jnp.where(labels[p] == tile * COLB + b, squares[p], 0.0)
            cover_out[tile, b] = found
        return 0

    lax.fori_loop(0, sky_count, cover, 0)

    def cover_copy(d):
        other = lax.rem(t + d, sky_count)
        return remote(cover_out.at[other], cover_in.at[d], cover_sems, (d,), other, f)

    def start_cover(d, _):
        cover_copy(d).start()
        return 0

    lax.fori_loop(1, sky_count, start_cover, 0)
    for o in ORIENTATIONS:
        for side in SIDES:
            wave(o, 1, side).start()

    def finish_labels(d, _):
        label_copy(d).wait_send()
        source = lax.rem(t - d + sky_count, sky_count)
        remote(label_ref, label_all.at[source], label_sems, (d,), source, f).wait_recv()
        return 0

    lax.fori_loop(1, sky_count, finish_labels, 0)
    to_scalars = pltpu.make_async_copy(label_all, label_s, local_sems.at[0])
    to_scalars.start()

    def finish_cover(d, _):
        cover_copy(d).wait()
        return 0

    lax.fori_loop(1, sky_count, finish_cover, 0)
    coverage = cover_out[t] + REGULARIZER
    for d in range(1, sky_count):
        coverage = coverage + cover_in[d]
    inverse[f] = 1.0 / coverage

    def inverse_copy(d):
        return remote(inverse.at[f], inverse.at[f], inverse_sems, (d,), t, lax.rem(f + d, freq_count))

    def start_inverse(d, _):
        inverse_copy(d).start()
        return 0

    lax.fori_loop(1, freq_count, start_inverse, 0)
    to_scalars.wait()

    def finish_inverse(d, _):
        inverse_copy(d).wait_send()
        source = lax.rem(f - d + freq_count, freq_count)
        remote(inverse.at[source], inverse.at[source], inverse_sems, (d,), t, source).wait_recv()
        return 0

    def sums(o, c, d, rows):
        base = at(1 - o, d) * COLB

        def source(j, found):
            sky = at(o, -j)
            found = list(found)
            for p in range(PIECES):
                value = held[c, j, p, rows, :].astype(F32)
                label = label_s[sky, p, 0]
                for b in range(COLB):
                    found[b] = found[b] + jnp.where(label == base + b, 1.0, 0.0) * value
            return tuple(found)

        return list(lax.fori_loop(0, SIDE, source, tuple(jnp.zeros((ROWS, BLK), F32) for _ in range(COLB))))

    def by_rows(body):
        def chunk(r, _):
            body(pl.ds(pl.multiple_of(r * ROWS, ROWS), ROWS), r)
            return 0

        lax.fori_loop(0, BLK // ROWS, chunk, 0)

    def main_copy(c, df):
        own = 2 * GROUP + c
        return remote(main.at[own], main.at[own - 2 * GROUP * df], main_sems, (c, (1 - df) // 2), t, f + df)

    def edge_copy(i, m):
        dt, df = EDGES[m]
        n = (1 - dt) // 2
        return remote(edge_out.at[i, n], edge_in.at[1 - df, i, n], edge_sems, (i, m), t + dt, f + df)

    def smooth(i):
        for m, (dt, df) in enumerate(EDGES):
            @pl.when(within(-dt, -df))
            def _():
                edge_copy(i, m).wait_recv()
        for df in SIDES:
            @pl.when(within(0, -df))
            def _():
                for o in ORIENTATIONS:
                    main_copy(o * GROUP + i, df).wait_recv()
        for g in range(3):
            for o in ORIENTATIONS:
                tall = jnp.concatenate(
                    [main[g * 2 * GROUP + o * GROUP + i], edge_in[g, i, 0], edge_in[g, i, 1]], axis=0
                )
                found = jnp.dot(down_ref[o], tall, preferred_element_type=F32).astype(BF16)
                spot = (2 * g + o) * BLK
                for k in range(KERNELS):
                    halfway[k, spot : spot + BLK, :] = found[k * BLK : (k + 1) * BLK]
        lane = lax.broadcasted_iota(jnp.int32, (6 * BLK, BLK), 1)
        for k in range(KERNELS):
            matrix = across_ref[k]
            found = [
                jnp.dot(halfway[k, :, n * BLK : n * BLK + WINDOW], matrix, preferred_element_type=F32)
                for n in range(3)
            ]
            columns = (
                found[0][:, :BLK],
                jnp.where(lane < BLK - RIM, found[0][:, BLK:], found[1][:, :BLK]),
                jnp.where(lane >= RIM, found[2][:, :BLK], found[1][:, BLK:]),
                found[2][:, BLK:],
            )
            for n, value in enumerate(columns):
                value = value.astype(BF16)
                for g in range(3):
                    for o in ORIENTATIONS:
                        spot = (2 * g + o) * BLK
                        smoothed[k, g * 2 * GROUP + o * GROUP + i, :, n * BLK : (n + 1) * BLK] = value[spot : spot + BLK]

    def step(n, _):
        @pl.when(n < GROUP)
        def _():
            for o in ORIENTATIONS:
                for side in SIDES:
                    wave(o, n, side).wait_recv()
                    onward(o, n, side).start()

        @pl.when(n < GROUP - 2)
        def _():
            for o in ORIENTATIONS:
                for side in SIDES:
                    wave(o, n + 2, side).start()

        @pl.when((n >= 1) & (n < GROUP + 1))
        def _():
            i = n - 1
            for o in ORIENTATIONS:
                c = o * GROUP + i
                for side in SIDES:
                    onward(o, i, side).wait_recv()

                def far(rows, r):
                    found = sums(o, c, 2, rows)
                    for b in range(COLB):
                        first_out[c, b // HALF, b % HALF, rows, :] = found[b].astype(BF16)

                by_rows(far)
                for side in SIDES:
                    first(o, i, side).start()

        @pl.when((n >= 2) & (n < GROUP + 2))
        def _():
            i = n - 2
            for o in ORIENTATIONS:
                c = o * GROUP + i
                for m, side in enumerate(SIDES):
                    first(o, i, side).wait_recv()

                    def near(rows, r):
                        found = sums(o, c, side, rows)
                        for b in range(HALF):
                            found[m * HALF + b] = found[m * HALF + b] + first_in[c, m, b, rows, :].astype(F32)
                        for b in range(COLB):
                            second_out[c, m, b, rows, :] = found[b].astype(BF16)

                    by_rows(near)
                    second(o, i, side).start()

        @pl.when(n == 3)
        def _():
            lax.fori_loop(1, freq_count, finish_inverse, 0)

        @pl.when((n >= 3) & (n < GROUP + 3))
        def _():
            i = n - 3
            for o in ORIENTATIONS:
                c = o * GROUP + i
                for side in SIDES:
                    second(o, i, side).wait_recv()

                def own(rows, r):
                    found = sums(o, c, 0, rows)
                    for b in range(COLB):
                        value = found[b]
                        for m in range(2):
                            value = value + second_in[c, m, b, rows, :].astype(F32)
                        scale = jnp.concatenate([inverse[r * (ROWS // 8) + q, b] for q in range(ROWS // 8)], axis=0)
                        main[2 * GROUP + c, rows, b * BLK : (b + 1) * BLK] = (value * scale).astype(BF16)

                by_rows(own)
                for df in SIDES:
                    @pl.when(within(0, df))
                    def _():
                        main_copy(c, df).start()
            ends = [
                [main[2 * GROUP + o * GROUP + i, rows, :].astype(F32) for o in ORIENTATIONS]
                for rows in (slice(BLK - NEAR, BLK), slice(0, NEAR))
            ]
            edge_out[i, 0] = jnp.concatenate([value[RIM:] for value in ends[0]], axis=0).astype(BF16)
            edge_out[i, 1] = jnp.concatenate([value[:RIM] for value in ends[1]], axis=0).astype(BF16)
            for m, (dt, df) in enumerate(EDGES):
                @pl.when(within(dt, df))
                def _():
                    edge_copy(i, m).start()

        @pl.when(n >= 4)
        def _():
            smooth(n - 4)

        return 0

    lax.fori_loop(0, GROUP + 4, step, 0)

    channels = 2 * GROUP
    total = channels + 2 * EDGE
    lane = lax.broadcasted_iota(jnp.int32, (channels, BLK), 1)
    power = jnp.zeros((channels, BLK), F32)
    chunks = (BLK // NEAR) * COLB

    def layers(k, i):
        rows = pl.ds(pl.multiple_of((i // COLB) * NEAR, NEAR), NEAR)
        columns = pl.ds(pl.multiple_of(lax.rem(i, COLB) * BLK, BLK), BLK)
        return rows, columns, [smoothed[k, c + 1, rows, columns].astype(F32) for c in range(total)]

    for k in range(KERNELS):
        acc[...] = jnp.zeros_like(acc)

        def energy(i, _):
            _, _, a = layers(k, i)
            for c, found in enumerate(box_sums(a)):
                for w, item in enumerate(found):
                    square = item * item
                    acc[w, c] += square[:8] + square[8:]
            return 0

        lax.fori_loop(0, chunks, energy, 0)
        for w in range(WIDTHS):
            value = jnp.sum(jnp.sum(acc[w], axis=1), axis=1, keepdims=True)
            power = jnp.where(lane == k * WIDTHS + w, value, power)
    power_out[...] = power

    def power_copy(d):
        return remote(power_out, power_in.at[d], power_sems, (d,), lax.rem(t + d, sky_count), f)

    def start_power(d, _):
        power_copy(d).start()
        return 0

    def finish_power(d, _):
        power_copy(d).wait()
        return 0

    lax.fori_loop(1, sky_count, start_power, 0)

    def drain(i, _):
        for o in ORIENTATIONS:
            for side in SIDES:
                for copy in (wave, onward, first, second):
                    copy(o, i, side).wait_send()
        for m, (dt, df) in enumerate(EDGES):
            @pl.when(within(dt, df))
            def _():
                edge_copy(i, m).wait_send()
        for df in SIDES:
            @pl.when(within(0, df))
            def _():
                for o in ORIENTATIONS:
                    main_copy(o * GROUP + i, df).wait_send()
        return 0

    lax.fori_loop(0, GROUP, drain, 0)
    clip = jnp.ones((channels, BLK), jnp.int32)
    for k in range(KERNELS):
        for w in range(WIDTHS):
            clip = jnp.where(lane == k * WIDTHS + w, clip_ref[k, w], clip)
    lax.fori_loop(1, sky_count, finish_power, 0)
    power = power_out[...]
    for d in range(1, sky_count):
        power = power + power_in[d]
    noise = jnp.sqrt(power * (1.0 / CELLS) + EPSILON)
    factor_v[...] = 10.0 / (clip.astype(F32) * noise)
    factors = pltpu.make_async_copy(factor_v, factor_s, local_sems.at[1])
    factors.start()
    factors.wait()

    def score(i, _):
        best = [None] * channels
        for k in range(KERNELS):
            rows, columns, a = layers(k, i)
            for c, found in enumerate(box_sums(a)):
                for w, item in enumerate(found):
                    value = jnp.abs(item) * factor_s[c, k * WIDTHS + w]
                    best[c] = value if best[c] is None else jnp.maximum(best[c], value)
        for c, item in enumerate(best):
            out_ref[c, rows, columns] = item
        return 0

    lax.fori_loop(0, chunks, score, 0)


def shards(pieces, beam, destination, clip_tenths):
    sky_count, freq_count = lax.axis_size("sky"), lax.axis_size("freq")
    piece_count, channels = pieces.shape[:2]
    across, down = band_constants()
    dma = pltpu.SemaphoreType.DMA
    plane = (BLK, BLK)
    row = COLB * BLK
    return pl.pallas_call(
        functools.partial(whole_kernel, sky_count, freq_count),
        out_shape=jax.ShapeDtypeStruct((channels, BLK, row), F32),
        in_specs=[
            pl.BlockSpec(memory_space=pl.ANY),
            pl.BlockSpec(memory_space=pl.ANY),
            pl.BlockSpec(memory_space=pltpu.SMEM),
            pl.BlockSpec(memory_space=pltpu.SMEM),
            pl.BlockSpec(memory_space=VMEM),
            pl.BlockSpec(memory_space=VMEM),
        ],
        out_specs=pl.BlockSpec(memory_space=VMEM),
        scratch_shapes=[
            VMEM(pieces.shape, BF16),
            VMEM(beam.shape, BF16),
            VMEM((piece_count, BLK), jnp.int32),
            VMEM((channels, SIDE, piece_count) + plane, BF16),
            VMEM((channels, 2, HALF) + plane, BF16),
            VMEM((channels, 2, HALF) + plane, BF16),
            VMEM((channels, 2, COLB) + plane, BF16),
            VMEM((channels, 2, COLB) + plane, BF16),
            VMEM((sky_count, piece_count, BLK), jnp.int32),
            pltpu.SMEM((sky_count, piece_count, BLK), jnp.int32),
            VMEM((sky_count, COLB, 8, BLK), F32),
            VMEM((sky_count, COLB, 8, BLK), F32),
            VMEM((freq_count, COLB, 8, BLK), F32),
            VMEM((3 * channels, BLK, row), BF16),
            VMEM((GROUP, 2, NEAR, row), BF16),
            VMEM((3, GROUP, 2, NEAR, row), BF16),
            VMEM((KERNELS, 6 * BLK, row), BF16),
            VMEM((KERNELS, 3 * channels, BLK, row), BF16),
            VMEM((WIDTHS, channels, 8, BLK), F32),
            VMEM((channels, BLK), F32),
            VMEM((sky_count, channels, BLK), F32),
            VMEM((channels, BLK), F32),
            pltpu.SMEM((channels, BLK), F32),
            dma((2,)),
            dma((2, sky_count)),
            dma((2,)),
            dma((2, sky_count)),
            dma((2, freq_count)),
            dma((2, channels, 2)),
            dma((2, channels, 2)),
            dma((2, channels, 2)),
            dma((2, channels, 2)),
            dma((2, channels, 2)),
            dma((2, GROUP, len(EDGES))),
            dma((2, sky_count)),
        ],
        compiler_params=pltpu.CompilerParams(
            collective_id=1, has_side_effects=True, vmem_limit_bytes=56 * 2**20
        ),
        name="whole",
    )(pieces, beam, destination, clip_tenths, across, down)


def solution(mesh):
    return jax.shard_map(
        shards,
        mesh=mesh,
        in_specs=(P("sky", "freq", None, None), P("sky", None, None), P("sky"), P()),
        out_specs=P("freq", "sky", None),
        check_vma=False,
    )
```

```python
import functools
import numpy as np
import ml_dtypes
import jax
import jax.numpy as jnp
from jax import lax
from jax.experimental import pallas as pl
from jax.experimental.pallas import tpu as pltpu
from jax.sharding import PartitionSpec as P

ROWB = 1
COLB = 4
BLK = 128
RIM = 8
EDGE = 7
KERNELS = 3
WIDTHS = 4
NEAR = 16
TALL = BLK + NEAR
REGULARIZER = 0.05
EPSILON = 1e-06
KERNEL_FWHM = (3.0, 6.0, 9.0)
HALF_WIDTHS = (0, 1, 3, 7)
CELLS = 2048 * 512
WINDOW = 256
MESH = pl.DeviceIdType.MESH
VMEM = pltpu.VMEM
F32 = jnp.float32
BF16 = jnp.bfloat16


def band_constants():
    across, down = [], []
    for fwhm in KERNEL_FWHM:
        offsets = np.arange(-RIM, RIM + 1).astype(np.float32)
        sigma = np.float32(fwhm / 2.3548)
        taps = np.exp(-offsets * offsets / (np.float32(2.0) * sigma * sigma)).astype(ml_dtypes.bfloat16)

        def pick(distance):
            inside = np.abs(distance) <= RIM
            return np.where(inside, taps[np.clip(distance + RIM, 0, 2 * RIM)], taps.dtype.type(0))

        columns = np.arange(WINDOW)
        across.append(pick(columns[:, None] - columns[None, :]))
        rows = np.arange(BLK)
        source = np.concatenate([rows, np.arange(-RIM, 0), BLK + np.arange(RIM)])
        down.append(pick(source[None, :] - rows[:, None]))
    return jnp.asarray(np.stack(across)), jnp.asarray(np.concatenate(down))


def box_sums(a):
    count = len(a) - 2 * EDGE
    two = {i: a[i] + a[i + 1] for i in range(4, 16)}
    three = {i: two[i] + a[i + 2] for i in range(6, 16)}
    four = {i: two[i] + two[i + 2] for i in range(4, 12)}
    own = four[7] + four[11]
    low = {6: a[6]}
    for i in range(5, -1, -1):
        low[i] = a[i] + low[i + 1]
    high = {1: a[15]}
    for i in range(2, 8):
        high[i] = high[i - 1] + a[i + 14]
    found = []
    for c in range(count):
        wide = own
        if c in low:
            wide = wide + low[c]
        if c in high:
            wide = wide + high[c]
        found.append((a[c + 7], three[c + 6], four[c + 4] + three[c + 8], wide))
    return found


SIDE = 4
GROUP = 4
PIECES = 8
DOUBLINGS = (1, 2, 4, 8)
HALF = COLB // 2
ROWS = 64
SIDES = (1, -1)
ORIENTATIONS = (0, 1)


def whole_kernel(
    sky_count, freq_count, pieces_hbm, beam_hbm, destination_ref, clip_ref, across_hbm, down_hbm, out_hbm,
    beam_ref, across_ref, down_ref, held, first_out, first_in, second_out, second_in, label_all, label_s,
    share, cover_out, cover_in, inverse, near_part, own_part, stage, spot_s, block_s, main, halfway, smoothed, acc, power_out, power_in,
    splat, out_ref,
    load_sems, label_sems, local_sems, share_sems, cover_sems, inverse_sems, wave_sems, hop_sems, first_sems,
    second_sems, main_sems, power_sems, out_sems,
):
    t, f = lax.axis_index("sky"), lax.axis_index("freq")
    x, y = t // SIDE, lax.rem(t, SIDE)
    barrier = pltpu.get_barrier_semaphore()

    def at(o, d):
        if o == 0:
            return lax.rem(x + d + SIDE, SIDE) * SIDE + y
        return x * SIDE + lax.rem(y + d + SIDE, SIDE)

    def remote(source, target, sems, where, sky, freq):
        return pltpu.make_async_remote_copy(
            src_ref=source, dst_ref=target, send_sem=sems.at[(0,) + where], recv_sem=sems.at[(1,) + where],
            device_id=(sky, freq), device_id_type=MESH,
        )

    def within(dt, df):
        good = None
        for value, delta, count in ((t, dt, sky_count), (f, df, freq_count)):
            if delta:
                here = value + delta
                one = (here >= 0) & (here < count)
                good = one if good is None else good & one
        return good

    def partner(size):
        return f + size * (1 - 2 * lax.rem(f // size, 2))

    def greet(sky, freq):
        pl.semaphore_signal(barrier, 1, device_id=(sky, freq), device_id_type=MESH)

    for o in ORIENTATIONS:
        for d in range(1, SIDE):
            greet(at(o, d), f)
    for size in DOUBLINGS:
        greet(t, partner(size))
    others = ((lax.rem(f, 2) == 1) & within(0, 1), (lax.rem(f, 2) == 0) & within(0, -1))
    more = jnp.int32(0)
    for here, df in ((others[0], 1), (others[1], -1)):
        more = more + here.astype(jnp.int32)

        @pl.when(here)
        def _():
            greet(t, f + df)

    load_beam = pltpu.make_async_copy(beam_hbm, beam_ref, load_sems.at[0])
    load_across = pltpu.make_async_copy(across_hbm, across_ref, load_sems.at[1])
    load_down = pltpu.make_async_copy(down_hbm, down_ref, load_sems.at[2])
    loads = [
        pltpu.make_async_copy(pieces_hbm.at[:, c], held.at[c, 0], load_sems.at[3 + c]) for c in range(2 * GROUP)
    ]
    load_beam.start()
    for load in loads:
        load.start()
    load_across.start()
    load_down.start()

    for p in range(PIECES):
        for o in ORIENTATIONS:
            label_all[o, 0, p : p + 1, :] = jnp.full((1, BLK), destination_ref[p], jnp.int32)

    for edge, g in ((f == 0, 0), (f == freq_count - 1, 2)):
        @pl.when(edge)
        def _():
            def clear(c, _):
                main[g * 2 * GROUP + c] = jnp.zeros(main.shape[1:], BF16)
                return 0

            lax.fori_loop(0, 2 * GROUP, clear, 0)

    load_beam.wait()
    pair = pl.ds(pl.multiple_of((f // 2) * NEAR, NEAR), NEAR)

    def mine(p):
        both = beam_ref[p, pair, :].astype(F32)
        return jnp.where(lax.rem(f, 2) == 0, both[:8], both[8:])

    for q in range(PIECES // 2):
        share[0, q] = jnp.concatenate([mine(2 * q), mine(2 * q + 1)], axis=0).astype(BF16)
    for load in loads:
        load.wait()

    def weigh(c, _):
        for p in range(PIECES):
            value = beam_ref[p].astype(F32) * held[c, 0, p].astype(F32)
            held[c, 0, p] = value.astype(BF16)
        return 0

    lax.fori_loop(0, 2 * GROUP, weigh, 0)
    pl.semaphore_wait(barrier, 2 * (SIDE - 1) + len(DOUBLINGS) + more)

    def channel_of(o, i):
        return GROUP + i if o else lax.rem(i + 1, GROUP)

    def wave(o, i, side):
        c = channel_of(o, i)
        n = (1 - side) // 2
        return remote(held.at[c, 0], held.at[c, 1 if side == 1 else 3], wave_sems, (c, n), at(o, side), f)

    def onward(o, i, side):
        c = channel_of(o, i)
        n = (1 - side) // 2
        half = pl.ds(n * (PIECES // 2), PIECES // 2)
        return remote(
            held.at[c, 1 if side == 1 else 3, half], held.at[c, 2, half], hop_sems, (c, n), at(o, side), f
        )

    def first(o, i, side):
        c = channel_of(o, i)
        n = (1 - side) // 2
        return remote(first_out.at[c, n], first_in.at[c, n], first_sems, (c, n), at(1 - o, side), f)

    def second(o, i, side):
        c = channel_of(o, i)
        n = (1 - side) // 2
        return remote(second_out.at[c, n], second_in.at[c, n], second_sems, (c, n), at(1 - o, side), f)

    def label_copy(o, d):
        return remote(label_all.at[o, 0], label_all.at[o, d], label_sems, (o, d), at(o, d), f)

    def share_copy(d):
        return remote(share.at[0], share.at[d], share_sems, (d,), at(0, d), f)

    for d in range(1, SIDE):
        share_copy(d).start()
        for o in ORIENTATIONS:
            label_copy(o, d).start()
    for o in ORIENTATIONS:
        for side in SIDES:
            wave(o, 0, side).start()

    for d in range(1, SIDE):
        for o in ORIENTATIONS:
            label_copy(o, d).wait()
        share_copy(d).wait()
    to_scalars = pltpu.make_async_copy(label_all, label_s, local_sems.at[0])
    to_scalars.start()

    aside = jnp.where(f < freq_count // 2, COLB, -COLB)

    def cover(d, _):
        base = at(1, d) * COLB
        found = [jnp.zeros((8, BLK), F32) for _ in range(2 * COLB)]
        for j in range(SIDE):
            for p in range(PIECES):
                value = share[j, p // 2].astype(F32)[(p % 2) * 8 : (p % 2) * 8 + 8]
                square = value * value
                label = jnp.broadcast_to(label_all[0, j, p : p + 1, :], (8, BLK))
                for b in range(COLB):
                    found[b] = found[b] + jnp.where(label == base + b, square, 0.0)
                    found[COLB + b] = found[COLB + b] + jnp.where(label == base + aside + b, square, 0.0)
        for b in range(2 * COLB):
            cover_out[d, b] = found[b]
        return 0

    lax.fori_loop(0, SIDE, cover, 0)

    def cover_copy(d):
        return remote(cover_out.at[d], cover_in.at[d], cover_sems, (d,), at(1, d), f)

    for d in range(1, SIDE):
        cover_copy(d).start()
    for o in ORIENTATIONS:
        for side in SIDES:
            wave(o, 1, side).start()
    for d in range(1, SIDE):
        cover_copy(d).wait()
    coverage = cover_out[0] + REGULARIZER
    for d in range(1, SIDE):
        coverage = coverage + cover_in[d]
    inverse[f] = 1.0 / coverage

    def spread(s, arrives):
        size = DOUBLINGS[s]
        other = partner(size)
        base = (other if arrives else f) // size * size
        span = inverse.at[pl.ds(base, size)]
        return remote(span, span, inverse_sems, (s,), t, other)

    spread(0, False).start()
    to_scalars.wait()
    load_across.wait()
    load_down.wait()

    for o in ORIENTATIONS:
        def tabulate(n, _):
            d, j = n // SIDE, lax.rem(n, SIDE)
            base = at(1 - o, d) * COLB
            spots = [jnp.int32(0), jnp.int32(0)]
            blocks = [jnp.int32(-1), jnp.int32(-1)]
            for p in range(PIECES):
                block = label_s[o, j, p, 0] - base
                inside = (block >= 0) & (block < COLB)
                again = inside & (blocks[0] >= 0)
                fresh = inside & (blocks[0] < 0)
                spots[1] = jnp.where(again, p, spots[1])
                blocks[1] = jnp.where(again, block, blocks[1])
                spots[0] = jnp.where(fresh, p, spots[0])
                blocks[0] = jnp.where(fresh, block, blocks[0])
            for k in range(2):
                spot_s[o, d, j, k] = spots[k]
                block_s[o, d, j, k] = blocks[k]
            return 0

        lax.fori_loop(0, SIDE * SIDE, tabulate, 0)

    def chosen(label, block):
        return jnp.where(label == block, 1.0, 0.0)

    def lay_out(o, c):
        def one(n, _):
            stage[o, n] = held[c, n // PIECES, lax.rem(n, PIECES)]
            return 0

        lax.fori_loop(0, SIDE * PIECES, one, 0)

    def sums(o, d, emit):
        base = at(1 - o, d) * COLB
        step_d = d % SIDE

        def chunk(r, _):
            rows = pl.ds(pl.multiple_of(r * ROWS, ROWS), ROWS)
            found = [jnp.zeros((ROWS, BLK), F32) for _ in range(COLB)]
            for j in range(SIDE):
                for k in range(2):
                    value = stage[o, j * PIECES + spot_s[o, step_d, j, k], rows, :].astype(F32)
                    label = block_s[o, step_d, j, k]
                    for b in range(COLB):
                        found[b] = found[b] + chosen(label, b) * value
            emit(rows, found, r)
            return 0

        lax.fori_loop(0, BLK // ROWS, chunk, 0)

        def beside(j, found):
            found = list(found)
            for p in range(PIECES):
                above = stage[o, j * PIECES + p, BLK - NEAR :, :].astype(F32)[RIM:]
                below = stage[o, j * PIECES + p, :NEAR, :].astype(F32)[:RIM]
                label = label_s[o, j, p, 0]
                for b in range(COLB):
                    found[b] = found[b] + chosen(label, base - COLB + b) * above
                    found[COLB + b] = found[COLB + b] + chosen(label, base + COLB + b) * below
            return tuple(found)

        found = lax.fori_loop(0, SIDE, beside, tuple(jnp.zeros((RIM, BLK), F32) for _ in range(2 * COLB)))
        emit(pl.ds(BLK, NEAR), [jnp.concatenate([found[b], found[COLB + b]], axis=0) for b in range(COLB)], None)

    def by_rows(body):
        def chunk(r, _):
            body(pl.ds(pl.multiple_of(r * ROWS, ROWS), ROWS), r)
            return 0

        lax.fori_loop(0, BLK // ROWS, chunk, 0)
        body(pl.ds(BLK, NEAR), None)

    def main_copy(o, i, df):
        c = channel_of(o, i)
        own = 2 * GROUP + c
        return remote(main.at[own], main.at[own - 2 * GROUP * df], main_sems, (c, (1 - df) // 2), t, f + df)

    def main_needed(o, i, df):
        return i < GROUP - 1 if o == (1 - df) // 2 else True

    def each_main(i, body, sign):
        for o in ORIENTATIONS:
            for df in SIDES:
                @pl.when(within(0, sign * df) & main_needed(o, i, df))
                def _():
                    body(main_copy(o, i, df))

    def smooth(i, chosen):
        for m, (g, o) in enumerate(chosen):
            tall = main[g * 2 * GROUP + channel_of(o, i)]
            found = jnp.dot(down_ref[...], tall, preferred_element_type=F32).astype(BF16)
            for k in range(KERNELS):
                halfway[k, m * BLK : (m + 1) * BLK, :] = found[k * BLK : (k + 1) * BLK]
        height = len(chosen) * BLK
        lane = lax.broadcasted_iota(jnp.int32, (height, BLK), 1)
        for k in range(KERNELS):
            matrix = across_ref[k]
            found = [
                jnp.dot(halfway[k, :height, n * BLK : n * BLK + WINDOW], matrix, preferred_element_type=F32)
                for n in range(3)
            ]
            columns = (
                found[0][:, :BLK],
                jnp.where(lane < BLK - RIM, found[0][:, BLK:], found[1][:, :BLK]),
                jnp.where(lane >= RIM, found[2][:, :BLK], found[1][:, BLK:]),
                found[2][:, BLK:],
            )
            for n, value in enumerate(columns):
                value = value.astype(BF16)
                for m, (g, o) in enumerate(chosen):
                    smoothed[k, g * 2 * GROUP + channel_of(o, i), :, n * BLK : (n + 1) * BLK] = (
                        value[m * BLK : (m + 1) * BLK]
                    )

    def wait_around(i):
        each_main(i, lambda copy: copy.wait_recv(), -1)

    def step(n, _):
        @pl.when(n < GROUP)
        def _():
            for o in ORIENTATIONS:
                for side in SIDES:
                    wave(o, n, side).wait_recv()
                    onward(o, n, side).start()

        @pl.when(n < GROUP - 2)
        def _():
            for o in ORIENTATIONS:
                for side in SIDES:
                    wave(o, n + 2, side).start()

        for s in range(len(DOUBLINGS)):
            @pl.when(n == s)
            def _():
                spread(s, False).wait_send()
                spread(s, True).wait_recv()
                if s + 1 < len(DOUBLINGS):
                    spread(s + 1, False).start()

        @pl.when(n >= 3)
        def _():
            i = n - 3
            for o in ORIENTATIONS:
                c = channel_of(o, i)
                for side in SIDES:
                    second(o, i, side).wait_recv()

                def own(rows, r):
                    for b in range(COLB):
                        value = own_part[o, b, rows, :]
                        for m in range(2):
                            value = value + second_in[c, m, b, rows, :].astype(F32)
                        if r is None:
                            scale = [inverse[freq_count - 1, COLB + b], inverse[0, COLB + b]]
                        else:
                            scale = [inverse[r * (ROWS // 8) + q, b] for q in range(ROWS // 8)]
                        value = value * jnp.concatenate(scale, axis=0)
                        main[2 * GROUP + c, rows, b * BLK : (b + 1) * BLK] = value.astype(BF16)

                by_rows(own)
            each_main(i, lambda copy: copy.start(), 1)

        @pl.when((n >= 2) & (n < GROUP + 2))
        def _():
            i = n - 2
            for o in ORIENTATIONS:
                c = channel_of(o, i)
                for m, side in enumerate(SIDES):
                    first(o, i, side).wait_recv()

                    def near(rows, r):
                        for b in range(COLB):
                            value = near_part[o, m, b, rows, :]
                            if b // HALF == m:
                                value = value + first_in[c, m, b % HALF, rows, :].astype(F32)
                            second_out[c, m, b, rows, :] = value.astype(BF16)

                    by_rows(near)
                    second(o, i, side).start()
            for o in ORIENTATIONS:
                def keep_own(rows, found, r):
                    for b in range(COLB):
                        own_part[o, b, rows, :] = found[b]

                sums(o, 0, keep_own)

        @pl.when((n >= 1) & (n < GROUP + 1))
        def _():
            i = n - 1
            for o in ORIENTATIONS:
                c = channel_of(o, i)
                for side in SIDES:
                    onward(o, i, side).wait_recv()

                def far(rows, found, r):
                    for b in range(COLB):
                        first_out[c, b // HALF, b % HALF, rows, :] = found[b].astype(BF16)

                lay_out(o, c)
                sums(o, 2, far)
                for side in SIDES:
                    first(o, i, side).start()
            for o in ORIENTATIONS:
                for m, side in enumerate(SIDES):
                    def keep_near(rows, found, r):
                        for b in range(COLB):
                            near_part[o, m, b, rows, :] = found[b]

                    sums(o, side, keep_near)

        @pl.when(n >= 3)
        def _():
            smooth(n - 3, ((1, 0), (1, 1)))

        @pl.when(n >= 4)
        def _():
            wait_around(n - 4)
            smooth(n - 4, ((0, 0), (0, 1), (2, 0), (2, 1)))

        return 0

    lax.fori_loop(0, GROUP + 3, step, 0)
    wait_around(GROUP - 1)
    smooth(GROUP - 1, ((0, 1), (2, 0)))

    channels = 2 * GROUP
    total = channels + 2 * EDGE
    lane = lax.broadcasted_iota(jnp.int32, (channels, BLK), 1)
    chunks = (BLK // NEAR) * COLB

    def layers(k, i):
        rows = pl.ds(pl.multiple_of((i // COLB) * NEAR, NEAR), NEAR)
        columns = pl.ds(pl.multiple_of(lax.rem(i, COLB) * BLK, BLK), BLK)
        return rows, columns, [smoothed[k, c + 1, rows, columns].astype(F32) for c in range(total)]

    def power_copy(k, o, d):
        return remote(power_out.at[k, o], power_in.at[k, o, d], power_sems, (k, o, d), at(o, d), f)

    def send_power(k, o, value):
        power_out[k, o] = value
        for d in range(1, SIDE):
            power_copy(k, o, d).start()

    def gathered(k, o):
        for d in range(1, SIDE):
            power_copy(k, o, d).wait()
        value = power_out[k, o]
        for d in range(1, SIDE):
            value = value + power_in[k, o, d]
        return value

    def take_power(k):
        acc[...] = jnp.zeros_like(acc)

        def energy(i, _):
            _, _, a = layers(k, i)
            for c, found in enumerate(box_sums(a)):
                for w, item in enumerate(found):
                    square = item * item
                    acc[w, c] += square[:8] + square[8:]
            return 0

        lax.fori_loop(0, chunks, energy, 0)
        power = jnp.zeros((channels, BLK), F32)
        for w in range(WIDTHS):
            value = jnp.sum(jnp.sum(acc[w], axis=1), axis=1, keepdims=True)
            power = jnp.where(lane == w, value, power)
        return power

    def take_scores(k):
        clip = jnp.ones((channels, BLK), jnp.int32)
        for w in range(WIDTHS):
            clip = jnp.where(lane == w, clip_ref[k, w], clip)
        noise = jnp.sqrt(gathered(k, 1) * (1.0 / CELLS) + EPSILON)
        factor = 10.0 / (clip.astype(F32) * noise)
        for c in range(channels):
            for w in range(WIDTHS):
                splat[c, w] = jnp.broadcast_to(factor[c : c + 1, w : w + 1], (8, BLK))

        def score(i, _):
            rows, columns, a = layers(k, i)
            for c, found in enumerate(box_sums(a)):
                best = None if k == 0 else out_ref[c, rows, columns].reshape(2, 8, BLK)
                for w, item in enumerate(found):
                    value = jnp.abs(item).reshape(2, 8, BLK) * splat[c, w]
                    best = value if best is None else jnp.maximum(best, value)
                out_ref[c, rows, columns] = best.reshape(NEAR, BLK)
            if k == KERNELS - 1:
                @pl.when(lax.rem(i, COLB) == COLB - 1)
                def _():
                    deliver(i // COLB).start()
            return 0

        lax.fori_loop(0, chunks, score, 0)

    def deliver(r):
        rows = pl.ds(pl.multiple_of(r * NEAR, NEAR), NEAR)
        return pltpu.make_async_copy(out_ref.at[:, rows], out_hbm.at[:, rows], out_sems.at[r])

    send_power(0, 0, take_power(0))
    power = take_power(1)
    send_power(0, 1, gathered(0, 0))
    send_power(1, 0, power)
    power = take_power(2)
    send_power(1, 1, gathered(1, 0))
    send_power(2, 0, power)
    take_scores(0)
    send_power(2, 1, gathered(2, 0))
    take_scores(1)

    def drain(i, _):
        for o in ORIENTATIONS:
            for side in SIDES:
                for copy in (wave, onward, first, second):
                    copy(o, i, side).wait_send()
        each_main(i, lambda copy: copy.wait_send(), 1)
        return 0

    lax.fori_loop(0, GROUP, drain, 0)
    take_scores(2)

    def delivered(r, _):
        deliver(r).wait()
        return 0

    lax.fori_loop(0, BLK // NEAR, delivered, 0)


def shards(pieces, beam, destination, clip_tenths):
    sky_count, freq_count = lax.axis_size("sky"), lax.axis_size("freq")
    piece_count, channels = pieces.shape[:2]
    across, down = band_constants()
    dma = pltpu.SemaphoreType.DMA
    plane, tall = (BLK, BLK), (TALL, BLK)
    row = COLB * BLK
    return pl.pallas_call(
        functools.partial(whole_kernel, sky_count, freq_count),
        out_shape=jax.ShapeDtypeStruct((channels, BLK, row), F32),
        in_specs=[
            pl.BlockSpec(memory_space=pl.ANY),
            pl.BlockSpec(memory_space=pl.ANY),
            pl.BlockSpec(memory_space=pltpu.SMEM),
            pl.BlockSpec(memory_space=pltpu.SMEM),
            pl.BlockSpec(memory_space=pl.ANY),
            pl.BlockSpec(memory_space=pl.ANY),
        ],
        out_specs=pl.BlockSpec(memory_space=pl.ANY),
        scratch_shapes=[
            VMEM(beam.shape, BF16),
            VMEM(across.shape, BF16),
            VMEM(down.shape, BF16),
            VMEM((channels, SIDE, piece_count) + plane, BF16),
            VMEM((channels, 2, HALF) + tall, BF16),
            VMEM((channels, 2, HALF) + tall, BF16),
            VMEM((channels, 2, COLB) + tall, BF16),
            VMEM((channels, 2, COLB) + tall, BF16),
            VMEM((2, SIDE, piece_count, BLK), jnp.int32),
            pltpu.SMEM((2, SIDE, piece_count, BLK), jnp.int32),
            VMEM((SIDE, piece_count // 2, NEAR, BLK), BF16),
            VMEM((SIDE, 2 * COLB, 8, BLK), F32),
            VMEM((SIDE, 2 * COLB, 8, BLK), F32),
            VMEM((freq_count, 2 * COLB, 8, BLK), F32),
            VMEM((2, 2, COLB) + tall, F32),
            VMEM((2, COLB) + tall, F32),
            VMEM((2, SIDE * piece_count) + plane, BF16),
            pltpu.SMEM((2, SIDE, SIDE, 2), jnp.int32),
            pltpu.SMEM((2, SIDE, SIDE, 2), jnp.int32),
            VMEM((3 * channels, TALL, row), BF16),
            VMEM((KERNELS, 4 * BLK, row), BF16),
            VMEM((KERNELS, 3 * channels, BLK, row), BF16),
            VMEM((WIDTHS, channels, 8, BLK), F32),
            VMEM((KERNELS, 2, channels, BLK), F32),
            VMEM((KERNELS, 2, SIDE, channels, BLK), F32),
            VMEM((channels, WIDTHS, 8, BLK), F32),
            VMEM((channels, BLK, row), F32),
            dma((3 + channels,)),
            dma((2, 2, SIDE)),
            dma((1,)),
            dma((2, SIDE)),
            dma((2, SIDE)),
            dma((2, len(DOUBLINGS))),
            dma((2, channels, 2)),
            dma((2, channels, 2)),
            dma((2, channels, 2)),
            dma((2, channels, 2)),
            dma((2, channels, 2)),
            dma((2, KERNELS, 2, SIDE)),
            dma((BLK // NEAR,)),
        ],
        compiler_params=pltpu.CompilerParams(
            collective_id=1, has_side_effects=True, vmem_limit_bytes=60 * 2**20
        ),
        name="whole",
    )(pieces, beam, destination, clip_tenths, across, down)


def solution(mesh):
    return jax.shard_map(
        shards,
        mesh=mesh,
        in_specs=(P("sky", "freq", None, None), P("sky", None, None), P("sky"), P()),
        out_specs=P("freq", "sky", None),
        check_vma=False,
    )
```

```python
import functools
import numpy as np
import ml_dtypes
import jax
import jax.numpy as jnp
from jax import lax
from jax.experimental import pallas as pl
from jax.experimental.pallas import tpu as pltpu
from jax.sharding import PartitionSpec as P

ROWB = 1
COLB = 4
BLK = 128
RIM = 8
EDGE = 7
KERNELS = 3
WIDTHS = 4
NEAR = 16
TALL = BLK + NEAR
REGULARIZER = 0.05
EPSILON = 1e-06
KERNEL_FWHM = (3.0, 6.0, 9.0)
HALF_WIDTHS = (0, 1, 3, 7)
CELLS = 2048 * 512
WINDOW = 256
MESH = pl.DeviceIdType.MESH
VMEM = pltpu.VMEM
F32 = jnp.float32
BF16 = jnp.bfloat16


def band_constants():
    across, down = [], []
    for fwhm in KERNEL_FWHM:
        offsets = np.arange(-RIM, RIM + 1).astype(np.float32)
        sigma = np.float32(fwhm / 2.3548)
        taps = np.exp(-offsets * offsets / (np.float32(2.0) * sigma * sigma)).astype(ml_dtypes.bfloat16)

        def pick(distance):
            inside = np.abs(distance) <= RIM
            return np.where(inside, taps[np.clip(distance + RIM, 0, 2 * RIM)], taps.dtype.type(0))

        columns = np.arange(WINDOW)
        across.append(pick(columns[:, None] - columns[None, :]))
        rows = np.arange(BLK)
        source = np.concatenate([rows, np.arange(-RIM, 0), BLK + np.arange(RIM)])
        down.append(pick(source[None, :] - rows[:, None]))
    return jnp.asarray(np.stack(across)), jnp.asarray(np.concatenate(down))


def box_sums(a):
    count = len(a) - 2 * EDGE
    two = {i: a[i] + a[i + 1] for i in range(4, 16)}
    three = {i: two[i] + a[i + 2] for i in range(6, 16)}
    four = {i: two[i] + two[i + 2] for i in range(4, 12)}
    own = four[7] + four[11]
    low = {6: a[6]}
    for i in range(5, -1, -1):
        low[i] = a[i] + low[i + 1]
    high = {1: a[15]}
    for i in range(2, 8):
        high[i] = high[i - 1] + a[i + 14]
    found = []
    for c in range(count):
        wide = own
        if c in low:
            wide = wide + low[c]
        if c in high:
            wide = wide + high[c]
        found.append((a[c + 7], three[c + 6], four[c + 4] + three[c + 8], wide))
    return found


SIDE = 4
GROUP = 4
PIECES = 8
DOUBLINGS = (1, 2, 4, 8)
HALF = COLB // 2
ROWS = 64
SIDES = (1, -1)
ORIENTATIONS = (0, 1)
ORDER = ((1, 2, 3, 0), (4, 5, 6, 7))


def whole_kernel(
    sky_count, freq_count, pieces_hbm, beam_hbm, destination_ref, clip_ref, across_hbm, down_hbm, out_hbm,
    beam_ref, across_ref, down_ref, held, first_out, first_in, second_out, second_in, label_all, label_s,
    share, cover_out, cover_in, inverse, near_part, own_part, stage, spot_s, block_s, main, halfway, smoothed, acc, power_out, power_in,
    splat, out_ref,
    load_sems, label_sems, local_sems, share_sems, cover_sems, inverse_sems, wave_sems, hop_sems, first_sems,
    second_sems, main_sems, power_sems, out_sems,
):
    t, f = lax.axis_index("sky"), lax.axis_index("freq")
    x, y = t // SIDE, lax.rem(t, SIDE)
    barrier = pltpu.get_barrier_semaphore()

    def at(o, d):
        if o == 0:
            return lax.rem(x + d + SIDE, SIDE) * SIDE + y
        return x * SIDE + lax.rem(y + d + SIDE, SIDE)

    def remote(source, target, sems, where, sky, freq):
        return pltpu.make_async_remote_copy(
            src_ref=source, dst_ref=target, send_sem=sems.at[(0,) + where], recv_sem=sems.at[(1,) + where],
            device_id=(sky, freq), device_id_type=MESH,
        )

    def within(dt, df):
        good = None
        for value, delta, count in ((t, dt, sky_count), (f, df, freq_count)):
            if delta:
                here = value + delta
                one = (here >= 0) & (here < count)
                good = one if good is None else good & one
        return good

    def partner(size):
        return f + size * (1 - 2 * lax.rem(f // size, 2))

    def greet(sky, freq):
        pl.semaphore_signal(barrier, 1, device_id=(sky, freq), device_id_type=MESH)

    for o in ORIENTATIONS:
        for d in range(1, SIDE):
            greet(at(o, d), f)
    for size in DOUBLINGS:
        greet(t, partner(size))
    others = ((lax.rem(f, 2) == 1) & within(0, 1), (lax.rem(f, 2) == 0) & within(0, -1))
    more = jnp.int32(0)
    for here, df in ((others[0], 1), (others[1], -1)):
        more = more + here.astype(jnp.int32)

        @pl.when(here)
        def _():
            greet(t, f + df)

    load_beam = pltpu.make_async_copy(beam_hbm, beam_ref, load_sems.at[0])
    load_across = pltpu.make_async_copy(across_hbm, across_ref, load_sems.at[1])
    load_down = pltpu.make_async_copy(down_hbm, down_ref, load_sems.at[2])
    loads = [
        pltpu.make_async_copy(pieces_hbm.at[:, c], held.at[c, 0], load_sems.at[3 + c]) for c in range(2 * GROUP)
    ]
    load_beam.start()
    for i in range(GROUP):
        for o in ORIENTATIONS:
            loads[ORDER[o][i]].start()
    load_across.start()
    load_down.start()

    for p in range(PIECES):
        for o in ORIENTATIONS:
            label_all[o, 0, p : p + 1, :] = jnp.full((1, BLK), destination_ref[p], jnp.int32)

    load_beam.wait()
    pair = pl.ds(pl.multiple_of((f // 2) * NEAR, NEAR), NEAR)

    def mine(p):
        both = beam_ref[p, pair, :].astype(F32)
        return jnp.where(lax.rem(f, 2) == 0, both[:8], both[8:])

    for q in range(PIECES // 2):
        share[0, q] = jnp.concatenate([mine(2 * q), mine(2 * q + 1)], axis=0).astype(BF16)

    def weigh(i):
        for o in ORIENTATIONS:
            loads[ORDER[o][i]].wait()

            def one(p, _):
                value = beam_ref[p].astype(F32) * held[ORDER[o][i], 0, p].astype(F32)
                held[ORDER[o][i], 0, p] = value.astype(BF16)
                return 0

            lax.fori_loop(0, PIECES, one, 0)

    weigh(0)
    pl.semaphore_wait(barrier, 2 * (SIDE - 1) + len(DOUBLINGS) + more)

    def channel_of(o, i):
        return GROUP + i if o else lax.rem(i + 1, GROUP)

    def wave(o, i, side):
        c = channel_of(o, i)
        n = (1 - side) // 2
        return remote(held.at[c, 0], held.at[c, 1 if side == 1 else 3], wave_sems, (c, n), at(o, side), f)

    def onward(o, i, side):
        c = channel_of(o, i)
        n = (1 - side) // 2
        half = pl.ds(n * (PIECES // 2), PIECES // 2)
        return remote(
            held.at[c, 1 if side == 1 else 3, half], held.at[c, 2, half], hop_sems, (c, n), at(o, side), f
        )

    def first(o, i, side):
        c = channel_of(o, i)
        n = (1 - side) // 2
        return remote(first_out.at[c, n], first_in.at[c, n], first_sems, (c, n), at(1 - o, side), f)

    def second(o, i, side):
        c = channel_of(o, i)
        n = (1 - side) // 2
        return remote(second_out.at[c, n], second_in.at[c, n], second_sems, (c, n), at(1 - o, side), f)

    def label_copy(o, d):
        return remote(label_all.at[o, 0], label_all.at[o, d], label_sems, (o, d), at(o, d), f)

    def share_copy(d):
        return remote(share.at[0], share.at[d], share_sems, (d,), at(0, d), f)

    for d in range(1, SIDE):
        share_copy(d).start()
        for o in ORIENTATIONS:
            label_copy(o, d).start()
    for o in ORIENTATIONS:
        for side in SIDES:
            wave(o, 0, side).start()

    for d in range(1, SIDE):
        for o in ORIENTATIONS:
            label_copy(o, d).wait()
        share_copy(d).wait()
    to_scalars = pltpu.make_async_copy(label_all, label_s, local_sems.at[0])
    to_scalars.start()

    aside = jnp.where(f < freq_count // 2, COLB, -COLB)

    def cover(d, _):
        base = at(1, d) * COLB
        found = [jnp.zeros((8, BLK), F32) for _ in range(2 * COLB)]
        for j in range(SIDE):
            for p in range(PIECES):
                value = share[j, p // 2].astype(F32)[(p % 2) * 8 : (p % 2) * 8 + 8]
                square = value * value
                label = jnp.broadcast_to(label_all[0, j, p : p + 1, :], (8, BLK))
                for b in range(COLB):
                    found[b] = found[b] + jnp.where(label == base + b, square, 0.0)
                    found[COLB + b] = found[COLB + b] + jnp.where(label == base + aside + b, square, 0.0)
        for b in range(2 * COLB):
            cover_out[d, b] = found[b]
        return 0

    lax.fori_loop(0, SIDE, cover, 0)

    def cover_copy(d):
        return remote(cover_out.at[d], cover_in.at[d], cover_sems, (d,), at(1, d), f)

    for d in range(1, SIDE):
        cover_copy(d).start()
    weigh(1)
    for o in ORIENTATIONS:
        for side in SIDES:
            wave(o, 1, side).start()
    weigh(2)
    weigh(3)

    for edge, g in ((f == 0, 0), (f == freq_count - 1, 2)):
        @pl.when(edge)
        def _():
            def clear(c, _):
                main[g * 2 * GROUP + c] = jnp.zeros(main.shape[1:], BF16)
                return 0

            lax.fori_loop(0, 2 * GROUP, clear, 0)

    for d in range(1, SIDE):
        cover_copy(d).wait()
    coverage = cover_out[0] + REGULARIZER
    for d in range(1, SIDE):
        coverage = coverage + cover_in[d]
    inverse[f] = 1.0 / coverage

    def spread(s, arrives):
        size = DOUBLINGS[s]
        other = partner(size)
        base = (other if arrives else f) // size * size
        span = inverse.at[pl.ds(base, size)]
        return remote(span, span, inverse_sems, (s,), t, other)

    spread(0, False).start()
    to_scalars.wait()
    load_across.wait()
    load_down.wait()

    for o in ORIENTATIONS:
        def tabulate(n, _):
            d, j = n // SIDE, lax.rem(n, SIDE)
            base = at(1 - o, d) * COLB
            spots = [jnp.int32(0), jnp.int32(0)]
            blocks = [jnp.int32(-1), jnp.int32(-1)]
            for p in range(PIECES):
                block = label_s[o, j, p, 0] - base
                inside = (block >= 0) & (block < COLB)
                again = inside & (blocks[0] >= 0)
                fresh = inside & (blocks[0] < 0)
                spots[1] = jnp.where(again, p, spots[1])
                blocks[1] = jnp.where(again, block, blocks[1])
                spots[0] = jnp.where(fresh, p, spots[0])
                blocks[0] = jnp.where(fresh, block, blocks[0])
            for k in range(2):
                spot_s[o, d, j, k] = spots[k]
                block_s[o, d, j, k] = blocks[k]
            return 0

        lax.fori_loop(0, SIDE * SIDE, tabulate, 0)

    def chosen(label, block):
        return jnp.where(label == block, 1.0, 0.0)

    def lay_out(o, c):
        def one(n, _):
            stage[o, n] = held[c, n // PIECES, lax.rem(n, PIECES)]
            return 0

        lax.fori_loop(0, SIDE * PIECES, one, 0)

    def sums(o, d, emit):
        base = at(1 - o, d) * COLB
        step_d = d % SIDE

        def chunk(r, _):
            rows = pl.ds(pl.multiple_of(r * ROWS, ROWS), ROWS)
            found = [jnp.zeros((ROWS, BLK), F32) for _ in range(COLB)]
            for j in range(SIDE):
                for k in range(2):
                    value = stage[o, j * PIECES + spot_s[o, step_d, j, k], rows, :].astype(F32)
                    label = block_s[o, step_d, j, k]
                    for b in range(COLB):
                        found[b] = found[b] + chosen(label, b) * value
            emit(rows, found, r)
            return 0

        lax.fori_loop(0, BLK // ROWS, chunk, 0)

        def beside(j, found):
            found = list(found)
            for p in range(PIECES):
                above = stage[o, j * PIECES + p, BLK - NEAR :, :].astype(F32)[RIM:]
                below = stage[o, j * PIECES + p, :NEAR, :].astype(F32)[:RIM]
                label = label_s[o, j, p, 0]
                for b in range(COLB):
                    found[b] = found[b] + chosen(label, base - COLB + b) * above
                    found[COLB + b] = found[COLB + b] + chosen(label, base + COLB + b) * below
            return tuple(found)

        found = lax.fori_loop(0, SIDE, beside, tuple(jnp.zeros((RIM, BLK), F32) for _ in range(2 * COLB)))
        emit(pl.ds(BLK, NEAR), [jnp.concatenate([found[b], found[COLB + b]], axis=0) for b in range(COLB)], None)

    def by_rows(body):
        def chunk(r, _):
            body(pl.ds(pl.multiple_of(r * ROWS, ROWS), ROWS), r)
            return 0

        lax.fori_loop(0, BLK // ROWS, chunk, 0)
        body(pl.ds(BLK, NEAR), None)

    def main_copy(o, i, df):
        c = channel_of(o, i)
        own = 2 * GROUP + c
        return remote(main.at[own], main.at[own - 2 * GROUP * df], main_sems, (c, (1 - df) // 2), t, f + df)

    def main_needed(o, i, df):
        return i < GROUP - 1 if o == (1 - df) // 2 else True

    def each_main(i, body, sign):
        for o in ORIENTATIONS:
            for df in SIDES:
                @pl.when(within(0, sign * df) & main_needed(o, i, df))
                def _():
                    body(main_copy(o, i, df))

    def smooth(i, chosen):
        for m, (g, o) in enumerate(chosen):
            tall = main[g * 2 * GROUP + channel_of(o, i)]
            found = jnp.dot(down_ref[...], tall, preferred_element_type=F32).astype(BF16)
            for k in range(KERNELS):
                halfway[k, m * BLK : (m + 1) * BLK, :] = found[k * BLK : (k + 1) * BLK]
        height = len(chosen) * BLK
        lane = lax.broadcasted_iota(jnp.int32, (height, BLK), 1)
        for k in range(KERNELS):
            matrix = across_ref[k]
            found = [
                jnp.dot(halfway[k, :height, n * BLK : n * BLK + WINDOW], matrix, preferred_element_type=F32)
                for n in range(3)
            ]
            columns = (
                found[0][:, :BLK],
                jnp.where(lane < BLK - RIM, found[0][:, BLK:], found[1][:, :BLK]),
                jnp.where(lane >= RIM, found[2][:, :BLK], found[1][:, BLK:]),
                found[2][:, BLK:],
            )
            for n, value in enumerate(columns):
                value = value.astype(BF16)
                for m, (g, o) in enumerate(chosen):
                    smoothed[k, g * 2 * GROUP + channel_of(o, i), :, n * BLK : (n + 1) * BLK] = (
                        value[m * BLK : (m + 1) * BLK]
                    )

    def wait_around(i):
        each_main(i, lambda copy: copy.wait_recv(), -1)

    def step(n, _):
        @pl.when(n < GROUP)
        def _():
            for o in ORIENTATIONS:
                for side in SIDES:
                    wave(o, n, side).wait_recv()
                    onward(o, n, side).start()

        @pl.when(n < GROUP - 2)
        def _():
            for o in ORIENTATIONS:
                for side in SIDES:
                    wave(o, n + 2, side).start()

        for s in range(len(DOUBLINGS)):
            @pl.when(n == s)
            def _():
                spread(s, False).wait_send()
                spread(s, True).wait_recv()
                if s + 1 < len(DOUBLINGS):
                    spread(s + 1, False).start()

        @pl.when(n >= 3)
        def _():
            i = n - 3
            for o in ORIENTATIONS:
                c = channel_of(o, i)
                for side in SIDES:
                    second(o, i, side).wait_recv()

                def own(rows, r):
                    for b in range(COLB):
                        value = own_part[o, b, rows, :]
                        for m in range(2):
                            value = value + second_in[c, m, b, rows, :].astype(F32)
                        if r is None:
                            scale = [inverse[freq_count - 1, COLB + b], inverse[0, COLB + b]]
                        else:
                            scale = [inverse[r * (ROWS // 8) + q, b] for q in range(ROWS // 8)]
                        value = value * jnp.concatenate(scale, axis=0)
                        main[2 * GROUP + c, rows, b * BLK : (b + 1) * BLK] = value.astype(BF16)

                by_rows(own)
            each_main(i, lambda copy: copy.start(), 1)

        @pl.when((n >= 2) & (n < GROUP + 2))
        def _():
            i = n - 2
            for o in ORIENTATIONS:
                c = channel_of(o, i)
                for m, side in enumerate(SIDES):
                    first(o, i, side).wait_recv()

                    def near(rows, r):
                        for b in range(COLB):
                            value = near_part[o, m, b, rows, :]
                            if b // HALF == m:
                                value = value + first_in[c, m, b % HALF, rows, :].astype(F32)
                            second_out[c, m, b, rows, :] = value.astype(BF16)

                    by_rows(near)
                    second(o, i, side).start()
            for o in ORIENTATIONS:
                def keep_own(rows, found, r):
                    for b in range(COLB):
                        own_part[o, b, rows, :] = found[b]

                sums(o, 0, keep_own)

        @pl.when((n >= 1) & (n < GROUP + 1))
        def _():
            i = n - 1
            for o in ORIENTATIONS:
                c = channel_of(o, i)
                for side in SIDES:
                    onward(o, i, side).wait_recv()

                def far(rows, found, r):
                    for b in range(COLB):
                        first_out[c, b // HALF, b % HALF, rows, :] = found[b].astype(BF16)

                lay_out(o, c)
                sums(o, 2, far)
                for side in SIDES:
                    first(o, i, side).start()
            for o in ORIENTATIONS:
                for m, side in enumerate(SIDES):
                    def keep_near(rows, found, r):
                        for b in range(COLB):
                            near_part[o, m, b, rows, :] = found[b]

                    sums(o, side, keep_near)

        @pl.when(n >= 3)
        def _():
            smooth(n - 3, ((1, 0), (1, 1)))

        @pl.when(n >= 4)
        def _():
            wait_around(n - 4)
            smooth(n - 4, ((0, 0), (0, 1), (2, 0), (2, 1)))

        return 0

    lax.fori_loop(0, GROUP + 3, step, 0)
    wait_around(GROUP - 1)
    smooth(GROUP - 1, ((0, 1), (2, 0)))

    channels = 2 * GROUP
    total = channels + 2 * EDGE
    lane = lax.broadcasted_iota(jnp.int32, (channels, BLK), 1)
    chunks = (BLK // NEAR) * COLB

    def layers(k, i):
        rows = pl.ds(pl.multiple_of((i // COLB) * NEAR, NEAR), NEAR)
        columns = pl.ds(pl.multiple_of(lax.rem(i, COLB) * BLK, BLK), BLK)
        return rows, columns, [smoothed[k, c + 1, rows, columns].astype(F32) for c in range(total)]

    def power_copy(k, o, d):
        return remote(power_out.at[k, o], power_in.at[k, o, d], power_sems, (k, o, d), at(o, d), f)

    def send_power(k, o, value):
        power_out[k, o] = value
        for d in range(1, SIDE):
            power_copy(k, o, d).start()

    def gathered(k, o):
        for d in range(1, SIDE):
            power_copy(k, o, d).wait()
        value = power_out[k, o]
        for d in range(1, SIDE):
            value = value + power_in[k, o, d]
        return value

    def take_power(k):
        acc[...] = jnp.zeros_like(acc)

        def energy(i, _):
            _, _, a = layers(k, i)
            for c, found in enumerate(box_sums(a)):
                for w, item in enumerate(found):
                    square = item * item
                    acc[w, c] += square[:8] + square[8:]
            return 0

        lax.fori_loop(0, chunks, energy, 0)
        power = jnp.zeros((channels, BLK), F32)
        for w in range(WIDTHS):
            value = jnp.sum(jnp.sum(acc[w], axis=1), axis=1, keepdims=True)
            power = jnp.where(lane == w, value, power)
        return power

    def take_scores(k):
        clip = jnp.ones((channels, BLK), jnp.int32)
        for w in range(WIDTHS):
            clip = jnp.where(lane == w, clip_ref[k, w], clip)
        noise = jnp.sqrt(gathered(k, 1) * (1.0 / CELLS) + EPSILON)
        factor = 10.0 / (clip.astype(F32) * noise)
        for c in range(channels):
            for w in range(WIDTHS):
                splat[c, w] = jnp.broadcast_to(factor[c : c + 1, w : w + 1], (8, BLK))

        def score(i, _):
            rows, columns, a = layers(k, i)
            for c, found in enumerate(box_sums(a)):
                best = None if k == 0 else out_ref[c, rows, columns].reshape(2, 8, BLK)
                for w, item in enumerate(found):
                    value = jnp.abs(item).reshape(2, 8, BLK) * splat[c, w]
                    best = value if best is None else jnp.maximum(best, value)
                out_ref[c, rows, columns] = best.reshape(NEAR, BLK)
            if k == KERNELS - 1:
                @pl.when(lax.rem(i, COLB) == COLB - 1)
                def _():
                    deliver(i // COLB).start()
            return 0

        lax.fori_loop(0, chunks, score, 0)

    def deliver(r):
        rows = pl.ds(pl.multiple_of(r * NEAR, NEAR), NEAR)
        return pltpu.make_async_copy(out_ref.at[:, rows], out_hbm.at[:, rows], out_sems.at[r])

    send_power(0, 0, take_power(0))
    power = take_power(1)
    send_power(0, 1, gathered(0, 0))
    send_power(1, 0, power)
    power = take_power(2)
    send_power(1, 1, gathered(1, 0))
    send_power(2, 0, power)
    take_scores(0)
    send_power(2, 1, gathered(2, 0))
    take_scores(1)

    def drain(i, _):
        for o in ORIENTATIONS:
            for side in SIDES:
                for copy in (wave, onward, first, second):
                    copy(o, i, side).wait_send()
        each_main(i, lambda copy: copy.wait_send(), 1)
        return 0

    lax.fori_loop(0, GROUP, drain, 0)
    take_scores(2)

    def delivered(r, _):
        deliver(r).wait()
        return 0

    lax.fori_loop(0, BLK // NEAR, delivered, 0)


def shards(pieces, beam, destination, clip_tenths):
    sky_count, freq_count = lax.axis_size("sky"), lax.axis_size("freq")
    piece_count, channels = pieces.shape[:2]
    across, down = band_constants()
    dma = pltpu.SemaphoreType.DMA
    plane, tall = (BLK, BLK), (TALL, BLK)
    row = COLB * BLK
    return pl.pallas_call(
        functools.partial(whole_kernel, sky_count, freq_count),
        out_shape=jax.ShapeDtypeStruct((channels, BLK, row), F32),
        in_specs=[
            pl.BlockSpec(memory_space=pl.ANY),
            pl.BlockSpec(memory_space=pl.ANY),
            pl.BlockSpec(memory_space=pltpu.SMEM),
            pl.BlockSpec(memory_space=pltpu.SMEM),
            pl.BlockSpec(memory_space=pl.ANY),
            pl.BlockSpec(memory_space=pl.ANY),
        ],
        out_specs=pl.BlockSpec(memory_space=pl.ANY),
        scratch_shapes=[
            VMEM(beam.shape, BF16),
            VMEM(across.shape, BF16),
            VMEM(down.shape, BF16),
            VMEM((channels, SIDE, piece_count) + plane, BF16),
            VMEM((channels, 2, HALF) + tall, BF16),
            VMEM((channels, 2, HALF) + tall, BF16),
            VMEM((channels, 2, COLB) + tall, BF16),
            VMEM((channels, 2, COLB) + tall, BF16),
            VMEM((2, SIDE, piece_count, BLK), jnp.int32),
            pltpu.SMEM((2, SIDE, piece_count, BLK), jnp.int32),
            VMEM((SIDE, piece_count // 2, NEAR, BLK), BF16),
            VMEM((SIDE, 2 * COLB, 8, BLK), F32),
            VMEM((SIDE, 2 * COLB, 8, BLK), F32),
            VMEM((freq_count, 2 * COLB, 8, BLK), F32),
            VMEM((2, 2, COLB) + tall, F32),
            VMEM((2, COLB) + tall, F32),
            VMEM((2, SIDE * piece_count) + plane, BF16),
            pltpu.SMEM((2, SIDE, SIDE, 2), jnp.int32),
            pltpu.SMEM((2, SIDE, SIDE, 2), jnp.int32),
            VMEM((3 * channels, TALL, row), BF16),
            VMEM((KERNELS, 4 * BLK, row), BF16),
            VMEM((KERNELS, 3 * channels, BLK, row), BF16),
            VMEM((WIDTHS, channels, 8, BLK), F32),
            VMEM((KERNELS, 2, channels, BLK), F32),
            VMEM((KERNELS, 2, SIDE, channels, BLK), F32),
            VMEM((channels, WIDTHS, 8, BLK), F32),
            VMEM((channels, BLK, row), F32),
            dma((3 + channels,)),
            dma((2, 2, SIDE)),
            dma((1,)),
            dma((2, SIDE)),
            dma((2, SIDE)),
            dma((2, len(DOUBLINGS))),
            dma((2, channels, 2)),
            dma((2, channels, 2)),
            dma((2, channels, 2)),
            dma((2, channels, 2)),
            dma((2, channels, 2)),
            dma((2, KERNELS, 2, SIDE)),
            dma((BLK // NEAR,)),
        ],
        compiler_params=pltpu.CompilerParams(
            collective_id=1, has_side_effects=True, vmem_limit_bytes=60 * 2**20
        ),
        name="whole",
    )(pieces, beam, destination, clip_tenths, across, down)


def solution(mesh):
    return jax.shard_map(
        shards,
        mesh=mesh,
        in_specs=(P("sky", "freq", None, None), P("sky", None, None), P("sky"), P()),
        out_specs=P("freq", "sky", None),
        check_vma=False,
    )
```
